32 devices in a mesh: gx: 4 (over y, core), gy: 8 (over z, x).
Axes of the slice: x: 2, y: 2, z: 4, core: 2. Of those that a mesh axis runs over, the one named last changes fastest.
Arguments:
- near_tiles: bfloat16 [4, 8, 32, 20, 128, 128], P('gx', 'gy'), may hold values from -0.125 to 0.125
- block: bfloat16 [4, 8, 4096, 64], P('gx', 'gy'), may hold values from -7 to 7, as said below
- adjacency: int32 [4, 8, 32, 20], P('gx', 'gy'), may hold values from 0 to 1023, as said below
Outputs:
- basis: float32 [4, 8, 4096, 64], P('gx', 'gy')
- r_factor: float32 [64, 64], replicated
The draws below stay inside these ranges and needn't reach their ends.
Inputs may be any that keep to these rules, and one draw needn't show every extreme that they name: `adjacency`: entry 0 of each row tile is the row tile itself; every entry names a tile of the device of its row tile or of a device whose gx and gy indices each differ by at most one, without wrapping. `block`: entries are real values of order one, within -7 to 7.
All inputs are finite; a program needn't handle non-finite values.
Results may differ from the reference program's by a relative error of at most 0.0003.
Values may be sent and summed in bfloat16 or wider, within the bound.
No kernel may reach another device: no remote copies, remote signals or barrier semaphores. Data moves between devices by JAX's collectives and lax.ppermute only.
A program may use at most 128 MiB of HBM per device.

```python
import jax
import jax.numpy as jnp
from jax import lax

K = 64
TILE = 128
NB = 20
TILES_DEV = 32
ROWS_DEV = 4096
ROWS = 131072
N_GX = 4
N_GY = 8


def draw_block(key, part):
    first, second, third = jax.random.split(jax.random.fold_in(key, 11), 3)
    shape = (N_GX, N_GY, ROWS_DEV, K)
    noise = jnp.clip(jax.random.normal(first, shape, jnp.float32), -4.0, 4.0)
    shared = jnp.clip(jax.random.normal(second, (N_GX, N_GY, ROWS_DEV, 1), jnp.float32), -4.0, 4.0)
    weights = jax.random.uniform(third, (K,), jnp.float32, 0.5, 1.5)
    return (0.7 * (noise + shared * weights)).astype(jnp.bfloat16)


def draw_adjacency(key, part):
    first, second, third = jax.random.split(jax.random.fold_in(key, 23), 3)
    shape = (N_GX, N_GY, TILES_DEV, NB)
    grid_x = lax.broadcasted_iota(jnp.int32, shape, 0)
    grid_y = lax.broadcasted_iota(jnp.int32, shape, 1)
    own_tile = lax.broadcasted_iota(jnp.int32, shape, 2)
    entry = lax.broadcasted_iota(jnp.int32, shape, 3)
    step_x = jax.random.randint(first, shape, -1, 2, jnp.int32)
    step_y = jax.random.randint(second, shape, -1, 2, jnp.int32)
    target_x = jnp.clip(grid_x + step_x, 0, N_GX - 1)
    target_y = jnp.clip(grid_y + step_y, 0, N_GY - 1)
    target_tile = jax.random.randint(third, shape, 0, TILES_DEV, jnp.int32)
    column = (target_x * N_GY + target_y) * TILES_DEV + target_tile
    diagonal = (grid_x * N_GY + grid_y) * TILES_DEV + own_tile
    return jnp.where(entry == 0, diagonal, column).astype(jnp.int32)


def steps_of(own_key, extent, cuts, smallest, high):
    loudness = 1.0
    for dim, shards_of in cuts:
        heights = jax.random.uniform(jax.random.fold_in(jax.random.fold_in(own_key, 6), dim), (shards_of,), jnp.float32, smallest / len(cuts), high / len(cuts))
        loudness = loudness * jnp.repeat(jnp.exp(heights), extent[dim] // shards_of).reshape((-1,) + (1,) * (len(extent) - 1 - dim))
    return loudness


def bell_draw(key, extent, spread, reach, cuts=(), kind=jnp.bfloat16):
    level = steps_of(key, extent, cuts, -0.22, 0.18) if cuts else 1.0
    array = jax.random.normal(key, extent, jnp.float32) * spread * level
    return jnp.minimum(jnp.maximum(array, -reach), reach).astype(kind)


def setup_inputs(seed: int = 0) -> dict:
    splits = jax.random.split(jax.random.key(seed), 4)
    return {
        "near_tiles": bell_draw(splits[0], (N_GX, N_GY, TILES_DEV, NB, TILE, TILE), (NB * TILE) ** -0.5, 0.125, ((0, 4), (1, 8))),
        "block": draw_block(jax.random.fold_in(splits[3], 71), 0),
        "adjacency": draw_adjacency(jax.random.fold_in(splits[3], 71), 0),
    }


def reference(near_tiles, block, adjacency):
    tiles_all = near_tiles.reshape(-1, NB, TILE, TILE)
    rows_all = block.reshape(-1, TILE, K)
    links = adjacency.reshape(-1, NB)

    def one_device(index):
        start = (index * TILES_DEV).astype(jnp.int32)
        tiles = lax.dynamic_slice_in_dim(tiles_all, start, TILES_DEV, 0).astype(jnp.float32)
        picks = lax.dynamic_slice_in_dim(links, start, TILES_DEV, 0)
        chosen = rows_all[picks].astype(jnp.float32)
        return jnp.einsum('rnij,rnjk->rik', tiles, chosen, precision=lax.Precision.HIGHEST)
    parts = lax.map(one_device, jnp.arange(N_GX * N_GY, dtype=jnp.int32))
    image = parts.reshape(-1, K)
    gram = jnp.dot(image.T, image, precision=lax.Precision.HIGHEST)
    upper = jnp.linalg.cholesky(gram).T
    ortho_t = jax.scipy.linalg.solve_triangular(upper.T, image.T, lower=True)
    scale = jnp.sqrt(jnp.float32(ROWS))
    basis = (ortho_t.T * scale).reshape(N_GX, N_GY, ROWS_DEV, K)
    return (basis, upper / scale)
```

```python
import functools

import jax
import jax.numpy as jnp
from jax import lax
from jax.experimental import pallas as pl
from jax.experimental.pallas import tpu as pltpu
from jax.sharding import PartitionSpec as P

UNROLL = 32
ROW_BY_ROW = (((1,), (1,)), ((), ()))
VMEM_LIMIT = 24 * 2**20


def pair_swap(value, axis):
    size = lax.axis_size(axis)
    return lax.ppermute(value, axis, [(i, i ^ 1) for i in range(size)])


def between_pairs(value, axis):
    size = lax.axis_size(axis)
    pairs = []
    for i in range(1, size - 1, 2):
        pairs += [(i, i + 1), (i + 1, i)]
    return lax.ppermute(value, axis, pairs)


def pass_on(value, axis):
    size = lax.axis_size(axis)
    pairs = [(i, i + 2) for i in range(0, size - 2, 2)]
    pairs += [(i, i - 2) for i in range(3, size, 2)]
    return lax.ppermute(value, axis, pairs)


def slot_of(owner, own):
    return jnp.where(owner == own, 0, jnp.where(owner == (own ^ 1), 1, 2))


def work_lists(links, tiles_dev, gy_count):
    count = links.size
    flat = links.T.reshape(-1)
    order = jnp.arange(count, dtype=jnp.int32)
    entry = (order % tiles_dev) * links.shape[1] + order // tiles_dev
    owner = flat // tiles_dev
    across = slot_of(owner // gy_count, lax.axis_index("gx"))
    phase = slot_of(owner % gy_count, lax.axis_index("gy"))
    zero_tile = 3 * tiles_dev
    code = entry * 128 + across * tiles_dev + flat % tiles_dev
    counts = jnp.stack([jnp.sum((phase == p).astype(jnp.int32)) for p in range(3)])
    steps = (counts + UNROLL - 1) // UNROLL
    starts = jnp.stack([0 * steps[0], steps[0], steps[0] + steps[1]])
    key = phase * count + order
    before = jnp.sum((key[None, :] < key[:, None]).astype(jnp.int32), axis=1)
    skipped = jnp.where(phase == 0, 0, jnp.where(phase == 1, counts[0], counts[0] + counts[1]))
    begin = jnp.where(phase == 0, starts[0], jnp.where(phase == 1, starts[1], starts[2]))
    place = before - skipped + begin * UNROLL
    length = count + 3 * UNROLL
    hits = place[None, :] == jnp.arange(length, dtype=jnp.int32)[:, None]
    listed = zero_tile + jnp.sum(jnp.where(hits, code[None, :] - zero_tile, 0), axis=1)
    return listed.astype(jnp.int32), jnp.concatenate([starts, steps]).astype(jnp.int32)


def accumulate(phase, listed, ranges, near, sources, acc, rows):
    tiles_dev, _, columns = acc.shape
    width = near.shape[-1]
    blocks = near.shape[0] // tiles_dev
    for slot, source in enumerate(sources):
        for tile in range(tiles_dev):
            rows[slot * tiles_dev + tile] = source[:, tile * width:(tile + 1) * width]
    rows[3 * tiles_dev] = jnp.zeros(rows.shape[1:], rows.dtype)
    start = ranges[phase]

    def step(index, carry):
        products = []
        for lane in range(UNROLL):
            code = listed[(start + index) * UNROLL + lane]
            entry = lax.shift_right_logical(code, 7)
            tile = rows[code & 127]
            product = lax.dot_general(near[entry], tile, ROW_BY_ROW, preferred_element_type=jnp.float32)
            products.append((lax.div(entry, blocks), product))
        for target, product in products:
            acc[target] += product
        return carry

    lax.fori_loop(0, ranges[3 + phase], step, 0)


def first_kernel(listed, ranges, near, own, core, outer, acc, rows):
    acc[...] = jnp.zeros(acc.shape, acc.dtype)
    accumulate(0, listed, ranges, near, (own, core, outer), acc, rows)


def next_kernel(phase, listed, ranges, near, own, core, outer, acc_in, acc, rows):
    accumulate(phase, listed, ranges, near, (own, core, outer), acc, rows)


def last_kernel(listed, ranges, near, own, core, outer, acc_in, split, gram, rows, acc):
    tiles_dev, width, columns = acc.shape
    acc[...] = acc_in[...]
    accumulate(2, listed, ranges, near, (own, core, outer), acc, rows)
    for tile in range(tiles_dev):
        image = acc[tile].T
        high = image.astype(jnp.bfloat16)
        low = (image - high.astype(jnp.float32)).astype(jnp.bfloat16)
        split[:, tile * width:(tile + 1) * width] = jnp.concatenate([high, low], axis=0)
    both = split[...]
    full = lax.dot_general(both, both, ROW_BY_ROW, preferred_element_type=jnp.float32)
    top = full[:columns, :columns] + full[columns:, columns:]
    side = full[:columns, columns:] + full[columns:, :columns]
    gram[...] = top + side


def finish_kernel(scale, gram, split, basis, factor):
    columns = gram.shape[0]
    row = lax.broadcasted_iota(jnp.int32, (columns, columns), 0)
    column = lax.broadcasted_iota(jnp.int32, (columns, columns), 1)
    unit = jnp.where(row == column, 1.0, 0.0)
    work = jnp.concatenate([gram[...], unit], axis=1)
    wide_row = lax.broadcasted_iota(jnp.int32, work.shape, 0)
    for k in range(columns - 1):
        begin = k // 8 * 8
        live = work[begin:]
        pivot_row = work[k:k + 1]
        pivot = pivot_row[:, k:k + 1]
        ratio = live[:, k:k + 1] * (1.0 / pivot)
        ratio = jnp.where(wide_row[begin:] > k, ratio, 0.0)
        live = live - ratio * pivot_row
        work = live if begin == 0 else jnp.concatenate([work[:begin], live], axis=0)
    left, right = work[:, :columns], work[:, columns:]
    diagonal = jnp.sum(jnp.where(row == column, left, 0.0), axis=1, keepdims=True)
    root = lax.rsqrt(diagonal)
    upper = jnp.where(row <= column, left, 0.0) * root
    factor[...] = upper * (1.0 / scale)
    weight = right * (root * scale)
    high = weight.astype(jnp.bfloat16)
    low = (weight - high.astype(jnp.float32)).astype(jnp.bfloat16)
    high_rows = split[:columns]
    stacked = jnp.concatenate([high, high, low], axis=1)
    values = jnp.concatenate([split[...], high_rows], axis=0)
    basis[...] = jnp.dot(stacked, values, preferred_element_type=jnp.float32)


def in_vmem():
    return pl.BlockSpec(memory_space=pltpu.VMEM)


def in_smem():
    return pl.BlockSpec(memory_space=pltpu.SMEM)


def sum_over_all(value):
    gx_count, gy_count = lax.axis_size("gx"), lax.axis_size("gy")
    total = gx_count * gy_count
    bits = [gy_count * 2**i for i in range(1, gx_count.bit_length() - 1)]
    bits = bits[:1] + [2**i for i in range(gy_count.bit_length() - 1)] + bits[1:]

    def from_other(mask):
        return lax.ppermute(value, ("gx", "gy"), [(i, i ^ mask) for i in range(total)])

    value = value + from_other(gy_count)
    while bits:
        taken, bits = bits[:2], bits[2:]
        near = value + from_other(taken[0])
        if len(taken) == 2:
            near = near + (from_other(taken[1]) + from_other(taken[0] ^ taken[1]))
        value = near
    return value


def shards(near_tiles, block, adjacency):
    tiles_dev, blocks = adjacency.shape[2:]
    width = near_tiles.shape[4]
    rows, columns = block.shape[2:]
    gx_count, gy_count = lax.axis_size("gx"), lax.axis_size("gy")
    scale = float(rows * gx_count * gy_count) ** 0.5

    beside = pair_swap(block, "gy")
    outer = between_pairs(block, "gx")
    core = pair_swap(block, "gx")
    beyond = pass_on(beside, "gy")
    beside_outer = between_pairs(beside, "gx")
    beside_core = pair_swap(beside, "gx")
    beyond_outer = between_pairs(beyond, "gx")
    beyond_core = pair_swap(beyond, "gx")

    listed, ranges = work_lists(adjacency[0, 0], tiles_dev, gy_count)
    near = near_tiles.reshape(tiles_dev * blocks, width, width)
    near = pltpu.with_memory_space_constraint(near, pltpu.VMEM)
    params = pltpu.CompilerParams(vmem_limit_bytes=VMEM_LIMIT)
    acc_shape = jax.ShapeDtypeStruct((tiles_dev, width, columns), jnp.float32)
    tile_rows = pltpu.VMEM((3 * tiles_dev + 1, columns, width), jnp.bfloat16)
    lists = [in_smem(), in_smem()]
    flat = lambda value: value[0, 0].T

    acc = pl.pallas_call(
        first_kernel, out_shape=acc_shape, in_specs=lists + [in_vmem()] * 4, out_specs=in_vmem(),
        scratch_shapes=[tile_rows], compiler_params=params, name="own_rows",
    )(listed, ranges, near, flat(block), flat(core), flat(outer))
    acc = pl.pallas_call(
        functools.partial(next_kernel, 1), out_shape=acc_shape, in_specs=lists + [in_vmem()] * 5, out_specs=in_vmem(),
        scratch_shapes=[tile_rows], compiler_params=params, name="beside_rows", input_output_aliases={6: 0},
    )(listed, ranges, near, flat(beside), flat(beside_core), flat(beside_outer), acc)
    split, gram = pl.pallas_call(
        last_kernel,
        out_shape=(
            jax.ShapeDtypeStruct((2 * columns, rows), jnp.bfloat16),
            jax.ShapeDtypeStruct((columns, columns), jnp.float32),
        ),
        in_specs=lists + [in_vmem()] * 5, out_specs=(in_vmem(), in_vmem()),
        scratch_shapes=[tile_rows, pltpu.VMEM(acc_shape.shape, jnp.float32)], compiler_params=params, name="beyond_rows",
    )(listed, ranges, near, flat(beyond), flat(beyond_core), flat(beyond_outer), acc)

    gram = sum_over_all(gram)
    basis, factor = pl.pallas_call(
        functools.partial(finish_kernel, scale),
        out_shape=(
            jax.ShapeDtypeStruct((columns, rows), jnp.float32),
            jax.ShapeDtypeStruct((columns, columns), jnp.float32),
        ),
        in_specs=[in_vmem()] * 2, out_specs=(in_vmem(), in_vmem()), compiler_params=params, name="orthonormalize",
    )(gram, split)
    return basis.T.reshape(1, 1, rows, columns), factor


def solution(mesh):
    in_specs = (
        P("gx", "gy", None, None, None, None),
        P("gx", "gy", None, None),
        P("gx", "gy", None, None),
    )
    out_specs = (P("gx", "gy", None, None), P())
    return jax.shard_map(shards, mesh=mesh, in_specs=in_specs, out_specs=out_specs, check_vma=False)
```

```python
import functools

import jax
import jax.numpy as jnp
from jax import lax
from jax.experimental import pallas as pl
from jax.experimental.pallas import tpu as pltpu
from jax.sharding import PartitionSpec as P

UNROLL = 32
PARTS = 4
LIST_ROWS = 6
PART_OF = (0, 1, 1, 1, 1, 2, 2, 3, 2)
SLOT_OF = (0, 0, 1, 2, 3, 0, 1, 0, 2)
ROW_BY_ROW = (((1,), (1,)), ((), ()))
VMEM_LIMIT = 8 * 2**20


def pair_swap(value, axis):
    size = lax.axis_size(axis)
    return lax.ppermute(value, axis, [(i, i ^ 1) for i in range(size)])


def between_pairs(value, axis):
    return lax.ppermute(value, axis, outside(lax.axis_size(axis)))


def outside(size):
    return [(i, i + 1) for i in range(1, size - 1, 2)] + [(i + 1, i) for i in range(1, size - 1, 2)]


def across_both(value):
    gx_count, gy_count = lax.axis_size("gx"), lax.axis_size("gy")
    pairs = [
        (from_x * gy_count + (from_y ^ 1), to_x * gy_count + to_y)
        for from_x, to_x in outside(gx_count)
        for from_y, to_y in outside(gy_count)
    ]
    return lax.ppermute(value, ("gx", "gy"), pairs)


def two_back(value, axis):
    size = lax.axis_size(axis)
    pairs = [(i, i - 2) for i in range(2, size, 2)]
    pairs += [(i, i + 2) for i in range(1, size - 2, 2)]
    return lax.ppermute(value, axis, pairs)


def exact_log2(value):
    assert value & (value - 1) == 0
    return value.bit_length() - 1


def look_up(table, index):
    packed = sum(value << (2 * place) for place, value in enumerate(table))
    return lax.shift_right_logical(jnp.full(index.shape, packed, jnp.int32), 2 * index) & 3


def build_lists(links, work, tiles_dev, blocks, gy_count):
    own_x, own_y = lax.axis_index("gx"), lax.axis_index("gy")
    count = links.shape[1]
    tile_bits, gy_bits = exact_log2(tiles_dev), exact_log2(gy_count)
    link = links[...]
    place = lax.broadcasted_iota(jnp.int32, link.shape, 1)
    owner = lax.shift_right_logical(link, tile_bits)
    owner_x, owner_y = lax.shift_right_logical(owner, gy_bits), owner & (gy_count - 1)
    across = jnp.where(owner_x == own_x, 0, jnp.where(owner_x == (own_x ^ 1), 1, 2))
    own_row, beside = owner_y == own_y, owner_y == (own_y ^ 1)
    kind = across + jnp.where(own_row, 0, jnp.where(beside, 3, 6))
    part, slot = look_up(PART_OF, kind), look_up(SLOT_OF, kind)
    entry = (place & (tiles_dev - 1)) * blocks + lax.shift_right_logical(place, tile_bits)
    code = entry * 512 + slot * tiles_dev + (link & (tiles_dev - 1)) + 1

    def ones_where(hit):
        return jnp.where(hit, 1.0, 0.0).astype(jnp.bfloat16)

    def iota(rows, dim):
        return lax.broadcasted_iota(jnp.int32, (rows, count), dim)

    is_part = iota(128, 0) == part
    earlier = ones_where(lax.broadcasted_iota(jnp.int32, (count, count), 0) < lax.broadcasted_iota(jnp.int32, (count, count), 1))
    before = jnp.dot(ones_where(is_part[:16]), earlier, preferred_element_type=jnp.float32)
    rank = jnp.sum(jnp.where(is_part[:16], before, 0.0), axis=0, keepdims=True).astype(jnp.int32)
    row = part * LIST_ROWS + lax.shift_right_logical(rank, 7)
    column_hits = ones_where(iota(128, 0) == (rank & 127))
    row_hits = iota(PARTS * LIST_ROWS + 2, 0) == row
    listed = jnp.zeros((PARTS * LIST_ROWS + 2, 128), jnp.float32)
    for shift in (16, 8, 0):
        digit = (lax.shift_right_logical(code, shift) & 255).astype(jnp.float32)
        values = jnp.where(row_hits, digit, 0.0).astype(jnp.bfloat16)
        listed = listed * 256.0 + lax.dot_general(values, column_hits, ROW_BY_ROW, preferred_element_type=jnp.float32)
    ones = jnp.ones((PARTS * LIST_ROWS + 2, count), jnp.bfloat16)
    lengths = lax.dot_general(ones, ones_where(is_part), ROW_BY_ROW, preferred_element_type=jnp.float32)
    line = lax.broadcasted_iota(jnp.int32, listed.shape, 0)
    work[...] = jnp.where(line == PARTS * LIST_ROWS + 1, lengths, listed).astype(jnp.int32)


def lay_out(sources, rows, tiles_dev):
    width = rows.shape[-1]
    rows[0] = jnp.zeros(rows.shape[1:], rows.dtype)
    for slot, source in enumerate(sources):
        for tile in range(tiles_dev):
            rows[1 + slot * tiles_dev + tile] = source[:, tile * width:(tile + 1) * width]


def accumulate(part, work, near, acc, rows):
    tiles_dev = acc.shape[0]
    blocks = near.shape[0] // tiles_dev
    groups = 128 // UNROLL

    def step(index, carry):
        line = part * LIST_ROWS + lax.div(index, groups)
        begin = lax.rem(index, groups) * UNROLL
        products = []
        for lane in range(UNROLL):
            code = work[line, begin + lane]
            entry = lax.shift_right_logical(code, 9)
            product = lax.dot_general(
                near[entry], rows[code & 511], ROW_BY_ROW, preferred_element_type=jnp.float32
            )
            products.append((lax.div(entry, blocks), product))
        for target, product in products:
            acc[target] += product
        return carry

    length = work[PARTS * LIST_ROWS + 1, part]
    lax.fori_loop(0, lax.div(length + (UNROLL - 1), UNROLL), step, 0)


def own_kernel(gy_count, links, near_hbm, own, acc, work, rows, near, work_smem, sems, work_sem):
    tiles_dev = acc.shape[0]
    chunks = sems.shape[0]
    length = near.shape[0] // chunks
    copies = [
        pltpu.make_async_copy(
            near_hbm.at[pl.ds(c * length, length)], near.at[pl.ds(c * length, length)], sems.at[c]
        )
        for c in range(chunks)
    ]
    for copy in copies:
        copy.start()
    build_lists(links, work, tiles_dev, near.shape[0] // tiles_dev, gy_count)
    work_copy = pltpu.make_async_copy(work, work_smem, work_sem)
    work_copy.start()
    lay_out((own,), rows, tiles_dev)
    acc[...] = jnp.zeros(acc.shape, acc.dtype)
    work_copy.wait()
    for copy in copies:
        copy.wait()
    accumulate(0, work_smem, near, acc, rows)


def middle_kernel(part, work, near, *refs):
    acc, rows = refs[-2:]
    lay_out(refs[:-3], rows, acc.shape[0])
    accumulate(part, work, near, acc, rows)


def last_kernel(work, near, source, acc_in, split, gram, rows, acc):
    tiles_dev, width, columns = acc.shape
    lay_out((source,), rows, tiles_dev)
    acc[...] = acc_in[...]
    accumulate(3, work, near, acc, rows)
    for tile in range(tiles_dev):
        image = acc[tile].T
        high = image.astype(jnp.bfloat16)
        low = (image - high.astype(jnp.float32)).astype(jnp.bfloat16)
        split[:, tile * width:(tile + 1) * width] = jnp.concatenate([high, low], axis=0)
    both = split[...]
    full = lax.dot_general(both, both, ROW_BY_ROW, preferred_element_type=jnp.float32)
    top = full[:columns, :columns] + full[columns:, columns:]
    side = full[:columns, columns:] + full[columns:, :columns]
    gram[...] = top + side


def finish_kernel(scale, gram, split, basis, factor):
    columns = gram.shape[0]
    row = lax.broadcasted_iota(jnp.int32, (columns, columns), 0)
    column = lax.broadcasted_iota(jnp.int32, (columns, columns), 1)
    unit = jnp.where(row == column, 1.0, 0.0)
    work = jnp.concatenate([gram[...], unit], axis=1)
    wide_row = lax.broadcasted_iota(jnp.int32, work.shape, 0)
    for k in range(columns - 1):
        begin = k // 8 * 8
        live = work[begin:]
        pivot_row = work[k:k + 1]
        pivot = pivot_row[:, k:k + 1]
        ratio = live[:, k:k + 1] * (1.0 / pivot)
        ratio = jnp.where(wide_row[begin:] > k, ratio, 0.0)
        live = live - ratio * pivot_row
        work = live if begin == 0 else jnp.concatenate([work[:begin], live], axis=0)
    left, right = work[:, :columns], work[:, columns:]
    diagonal = jnp.sum(jnp.where(row == column, left, 0.0), axis=1, keepdims=True)
    root = lax.rsqrt(diagonal)
    upper = jnp.where(row <= column, left, 0.0) * root
    factor[...] = upper * (1.0 / scale)
    weight = right * (root * scale)
    high = weight.astype(jnp.bfloat16)
    low = (weight - high.astype(jnp.float32)).astype(jnp.bfloat16)
    high_rows = split[:columns]
    stacked = jnp.concatenate([high, high, low], axis=1)
    values = jnp.concatenate([split[...], high_rows], axis=0)
    basis[...] = jnp.dot(stacked, values, preferred_element_type=jnp.float32)


def in_vmem():
    return pl.BlockSpec(memory_space=pltpu.VMEM)


def in_smem():
    return pl.BlockSpec(memory_space=pltpu.SMEM)


def sum_over_all(value):
    gx_count, gy_count = lax.axis_size("gx"), lax.axis_size("gy")
    total = gx_count * gy_count
    bits = [gy_count * 2**i for i in range(1, gx_count.bit_length() - 1)]
    bits = bits[:1] + [2**i for i in range(gy_count.bit_length() - 1)] + bits[1:]

    def from_other(mask):
        return lax.ppermute(value, ("gx", "gy"), [(i, i ^ mask) for i in range(total)])

    value = value + from_other(gy_count)
    while bits:
        taken, bits = bits[:2], bits[2:]
        near = value + from_other(taken[0])
        if len(taken) == 2:
            near = near + (from_other(taken[1]) + from_other(taken[0] ^ taken[1]))
        value = near
    return value


def shards(near_tiles, block, adjacency):
    tiles_dev, blocks = adjacency.shape[2:]
    width = near_tiles.shape[4]
    rows, columns = block.shape[2:]
    gx_count, gy_count = lax.axis_size("gx"), lax.axis_size("gy")
    scale = float(rows * gx_count * gy_count) ** 0.5

    beside = pair_swap(block, "gy")
    two_off = two_back(block, "gy")
    outer = between_pairs(block, "gx")
    core = pair_swap(block, "gx")

    count = tiles_dev * blocks
    links = adjacency[0, 0].T.reshape(1, -1)
    near = near_tiles.reshape(count, width, width)
    acc_shape = jax.ShapeDtypeStruct((tiles_dev, width, columns), jnp.float32)
    flat = lambda value: value[0, 0].T

    def tile_rows(sources):
        return pltpu.VMEM((sources * tiles_dev + 1, columns, width), jnp.bfloat16)

    def params(limit=VMEM_LIMIT):
        return dict(
            compiler_params=pltpu.CompilerParams(vmem_limit_bytes=limit),
        )

    acc, work = pl.pallas_call(
        functools.partial(own_kernel, gy_count),
        out_shape=(acc_shape, jax.ShapeDtypeStruct((PARTS * LIST_ROWS + 2, 128), jnp.int32)),
        in_specs=[in_vmem(), pl.BlockSpec(memory_space=pltpu.HBM), in_vmem()],
        out_specs=(in_vmem(), in_vmem()),
        scratch_shapes=[
            tile_rows(1),
            pltpu.VMEM(near.shape, near.dtype),
            pltpu.SMEM((PARTS * LIST_ROWS + 2, 128), jnp.int32),
            pltpu.SemaphoreType.DMA((8,)),
            pltpu.SemaphoreType.DMA,
        ],
        name="own_rows", **params(46 * 2**20),
    )(links, near, flat(block))
    near = pltpu.with_memory_space_constraint(near, pltpu.VMEM)

    def add(part, acc, *sources):
        return pl.pallas_call(
            functools.partial(middle_kernel, part), out_shape=acc_shape, out_specs=in_vmem(),
            in_specs=[in_smem()] + [in_vmem()] * (2 + len(sources)), scratch_shapes=[tile_rows(len(sources))],
            name=f"rows_{part}", input_output_aliases={2 + len(sources): 0}, **params(),
        )(work, near, *(flat(source) for source in sources), acc)

    beside, two_off, outer, core, acc = lax.optimization_barrier((beside, two_off, outer, core, acc))
    beyond = pair_swap(two_off, "gy")
    beside_outer = between_pairs(beside, "gx")
    beyond_outer = across_both(beside)
    beside_core = pair_swap(beside, "gx")
    acc = add(1, acc, core, outer, beside, beside_core)
    beyond, beside_outer, beyond_outer, acc = lax.optimization_barrier((beyond, beside_outer, beyond_outer, acc))
    beyond_core = pair_swap(beyond, "gx")
    acc = add(2, acc, beside_outer, beyond, beyond_outer)
    split, gram = pl.pallas_call(
        last_kernel,
        out_shape=(
            jax.ShapeDtypeStruct((2 * columns, rows), jnp.bfloat16),
            jax.ShapeDtypeStruct((columns, columns), jnp.float32),
        ),
        in_specs=[in_smem()] + [in_vmem()] * 3, out_specs=(in_vmem(), in_vmem()),
        scratch_shapes=[tile_rows(1), pltpu.VMEM(acc_shape.shape, jnp.float32)], name="rows_3_and_gram", **params(),
    )(work, near, flat(beyond_core), acc)

    gram = sum_over_all(gram)
    basis, factor = pl.pallas_call(
        functools.partial(finish_kernel, scale),
        out_shape=(
            jax.ShapeDtypeStruct((columns, rows), jnp.float32),
            jax.ShapeDtypeStruct((columns, columns), jnp.float32),
        ),
        in_specs=[in_vmem()] * 2, out_specs=(in_vmem(), in_vmem()), name="orthonormalize", **params(),
    )(gram, split)
    return basis.T.reshape(1, 1, rows, columns), factor


def solution(mesh):
    in_specs = (
        P("gx", "gy", None, None, None, None),
        P("gx", "gy", None, None),
        P("gx", "gy", None, None),
    )
    out_specs = (P("gx", "gy", None, None), P())
    return jax.shard_map(shards, mesh=mesh, in_specs=in_specs, out_specs=out_specs, check_vma=False)
```

```python
import functools

import jax
import jax.numpy as jnp
from jax import lax
from jax.experimental import pallas as pl
from jax.experimental.pallas import tpu as pltpu
from jax.sharding import PartitionSpec as P

UNROLL = 32
EARLY = 3
CHUNKS = 8
PARTS = 4
LIST_ROWS = 6
PART_OF = (0, 1, 1, 1, 1, 2, 2, 3, 2)
SLOT_OF = (0, 0, 1, 2, 3, 0, 1, 0, 2)
ROW_BY_ROW = (((1,), (1,)), ((), ()))
VMEM_LIMIT = 8 * 2**20


def pair_swap(value, axis):
    size = lax.axis_size(axis)
    return lax.ppermute(value, axis, [(i, i ^ 1) for i in range(size)])


def between_pairs(value, axis):
    return lax.ppermute(value, axis, outside(lax.axis_size(axis)))


def outside(size):
    return [(i, i + 1) for i in range(1, size - 1, 2)] + [(i + 1, i) for i in range(1, size - 1, 2)]


def across_both(value):
    gx_count, gy_count = lax.axis_size("gx"), lax.axis_size("gy")
    pairs = [
        (from_x * gy_count + (from_y ^ 1), to_x * gy_count + to_y)
        for from_x, to_x in outside(gx_count)
        for from_y, to_y in outside(gy_count)
    ]
    return lax.ppermute(value, ("gx", "gy"), pairs)


def two_back(value, axis):
    size = lax.axis_size(axis)
    pairs = [(i, i - 2) for i in range(2, size, 2)]
    pairs += [(i, i + 2) for i in range(1, size - 2, 2)]
    return lax.ppermute(value, axis, pairs)


def exact_log2(value):
    assert value & (value - 1) == 0
    return value.bit_length() - 1


def look_up(table, index):
    packed = sum(value << (2 * place) for place, value in enumerate(table))
    return lax.shift_right_logical(jnp.full(index.shape, packed, jnp.int32), 2 * index) & 3


def build_lists(links, work, tiles_dev, blocks, gy_count):
    own_x, own_y = lax.axis_index("gx"), lax.axis_index("gy")
    count = links.shape[1]
    tile_bits, gy_bits = exact_log2(tiles_dev), exact_log2(gy_count)
    link = links[...]
    place = lax.broadcasted_iota(jnp.int32, link.shape, 1)
    owner = lax.shift_right_logical(link, tile_bits)
    owner_x, owner_y = lax.shift_right_logical(owner, gy_bits), owner & (gy_count - 1)
    across = jnp.where(owner_x == own_x, 0, jnp.where(owner_x == (own_x ^ 1), 1, 2))
    own_row, beside = owner_y == own_y, owner_y == (own_y ^ 1)
    kind = across + jnp.where(own_row, 0, jnp.where(beside, 3, 6))
    part, slot = look_up(PART_OF, kind), look_up(SLOT_OF, kind)
    code = place * 512 + slot * tiles_dev + (link & (tiles_dev - 1)) + 1

    def ones_where(hit):
        return jnp.where(hit, 1.0, 0.0).astype(jnp.bfloat16)

    def iota(shape, dim):
        return lax.broadcasted_iota(jnp.int32, shape, dim)

    def dot(left, right):
        return jnp.dot(left, right, preferred_element_type=jnp.float32)

    def row_dot(left, right):
        return lax.dot_general(left, right, ROW_BY_ROW, preferred_element_type=jnp.float32)

    def to_even(length):
        return ((length.astype(jnp.int32) + 1) & -2).astype(jnp.float32).astype(jnp.bfloat16)

    groups, lines = PARTS * tiles_dev, PARTS * LIST_ROWS + 2
    group = part * tiles_dev + lax.div(place, blocks)
    in_group = iota((groups, count), 0) == group
    members = ones_where(in_group)
    before = dot(members, ones_where(iota((count, count), 0) < iota((count, count), 1)))
    lengths = dot(members, jnp.ones((count, 128), jnp.bfloat16))
    first, second = iota((groups, groups), 0), iota((groups, groups), 1)
    same_part = lax.shift_right_logical(first, tile_bits) == lax.shift_right_logical(second, tile_bits)
    starts = dot(ones_where(same_part & (second < first)), to_even(lengths))
    rank = jnp.sum(jnp.where(in_group, before + starts[:, :1], 0.0), axis=0, keepdims=True).astype(jnp.int32)
    row = part * LIST_ROWS + lax.shift_right_logical(rank, 7)
    column_hits = ones_where(iota((128, count), 0) == (rank & 127))
    row_hits = iota((lines, count), 0) == row
    listed = jnp.zeros((lines, 128), jnp.float32)
    for shift in (16, 8, 0):
        digit = (lax.shift_right_logical(code, shift) & 255).astype(jnp.float32)
        listed = listed * 256.0 + row_dot(jnp.where(row_hits, digit, 0.0).astype(jnp.bfloat16), column_hits)
    by_group = to_even(row_dot(jnp.ones((lines, count), jnp.bfloat16), members))
    of_part = iota((128, groups), 0) == lax.shift_right_logical(iota((128, groups), 1), tile_bits)
    totals = row_dot(by_group, ones_where(of_part))
    work[...] = jnp.where(iota((lines, 128), 0) == lines - 1, totals, listed).astype(jnp.int32)


def lay_out(sources, rows, tiles_dev):
    width = rows.shape[-1]
    rows[0] = jnp.zeros(rows.shape[1:], rows.dtype)
    for slot, source in enumerate(sources):
        for tile in range(tiles_dev):
            rows[1 + slot * tiles_dev + tile] = source[:, tile * width:(tile + 1) * width]


def batches(part, work):
    return lax.div(work[PARTS * LIST_ROWS + 1, part] + (UNROLL - 1), UNROLL)


def code_at(part, work, index, lane):
    groups = 128 // UNROLL
    return work[part * LIST_ROWS + lax.div(index, groups), lax.rem(index, groups) * UNROLL + lane]


def entry_of(code):
    return lax.shift_right_logical(code, 9)


def add_batch(part, work, index, tile_of, blocks, acc, rows):
    products = []
    for lane in range(0, UNROLL, 2):
        codes = [code_at(part, work, index, lane + i) for i in range(2)]
        entries = [entry_of(code) for code in codes]
        left = jnp.concatenate([tile_of(entry, lane + i) for i, entry in enumerate(entries)], axis=1)
        right = jnp.concatenate([rows[code & 511] for code in codes], axis=1)
        product = lax.dot_general(left, right, ROW_BY_ROW, preferred_element_type=jnp.float32)
        products.append((lax.div(entries[0], blocks), product))
    for target, product in products:
        acc[target] += product


def accumulate(part, work, near, acc, rows, first=0):
    blocks = near.shape[0] // acc.shape[0]

    def step(index, carry):
        add_batch(part, work, index, lambda entry, lane: near[entry], blocks, acc, rows)
        return carry

    lax.fori_loop(first, batches(part, work), step, 0)


def own_kernel(gy_count, links, near_hbm, own, acc, work, rows, tiles, work_smem, sems, work_sem):
    tiles_dev = acc.shape[0]
    blocks = near_hbm.shape[0] // tiles_dev
    build_lists(links, work, tiles_dev, blocks, gy_count)
    work_copy = pltpu.make_async_copy(work, work_smem, work_sem)
    work_copy.start()
    lay_out((own,), rows, tiles_dev)
    acc[...] = jnp.zeros(acc.shape, acc.dtype)
    work_copy.wait()
    count = jnp.minimum(batches(0, work_smem), EARLY)

    def fetch(index, carry):
        for lane in range(UNROLL):
            entry = entry_of(code_at(0, work_smem, index, lane))
            pltpu.make_async_copy(near_hbm.at[entry], tiles.at[index * UNROLL + lane], sems.at[index]).start()
        return carry

    def step(index, carry):
        held = tiles.at[pl.ds(index * UNROLL, UNROLL)]
        pltpu.make_async_copy(near_hbm.at[pl.ds(0, UNROLL)], held, sems.at[index]).wait()
        add_batch(0, work_smem, index, lambda entry, lane: held[lane], blocks, acc, rows)
        return carry

    lax.fori_loop(0, count, fetch, 0)
    lax.fori_loop(0, count, step, 0)


def middle_kernel(part, work, near, *refs):
    acc, rows = refs[-2:]
    lay_out(refs[:-3], rows, acc.shape[0])
    accumulate(part, work, near, acc, rows)


def loading_kernel(work, near_hbm, *refs):
    near, acc, rows, own_rows, sems = refs[-5:]
    sources = refs[:-6]
    tiles_dev = acc.shape[0]
    blocks = near.shape[0] // tiles_dev
    chunks = sems.shape[0]
    length = near.shape[0] // chunks

    def load(chunk):
        held = pl.ds(chunk * length, length)
        return pltpu.make_async_copy(near_hbm.at[held], near.at[held], sems.at[chunk])

    for chunk in range(chunks):
        load(chunk).start()
    lay_out(sources[1:], rows, tiles_dev)
    count = batches(1, work)

    def wait(chunk, carry):
        load(chunk).wait()
        return carry

    def step(index, there):
        last = lax.div(entry_of(code_at(1, work, index, UNROLL - 2)), length)
        needed = jnp.where(index == count - 1, chunks, last + 1)
        lax.fori_loop(there, needed, wait, 0)
        add_batch(1, work, index, lambda entry, lane: near[entry], blocks, acc, rows)
        return jnp.maximum(there, needed)

    there = lax.fori_loop(0, count, step, jnp.int32(0))
    lax.fori_loop(there, chunks, wait, 0)
    lay_out(sources[:1], own_rows, tiles_dev)
    accumulate(0, work, near, acc, own_rows, EARLY)


def last_kernel(work, near, source, acc_in, split, gram, rows, acc):
    tiles_dev, width, columns = acc.shape
    lay_out((source,), rows, tiles_dev)
    acc[...] = acc_in[...]
    accumulate(3, work, near, acc, rows)
    for tile in range(tiles_dev):
        image = acc[tile].T
        high = image.astype(jnp.bfloat16)
        low = (image - high.astype(jnp.float32)).astype(jnp.bfloat16)
        split[:, tile * width:(tile + 1) * width] = jnp.concatenate([high, low], axis=0)
    both = split[...]
    full = lax.dot_general(both, both, ROW_BY_ROW, preferred_element_type=jnp.float32)
    top = full[:columns, :columns] + full[columns:, columns:]
    side = full[:columns, columns:] + full[columns:, :columns]
    gram[...] = top + side


def finish_kernel(scale, gram, split, basis, factor):
    columns = gram.shape[0]
    shape = (8, 2 * columns)
    row = lax.broadcasted_iota(jnp.int32, shape, 0)
    lane = lax.broadcasted_iota(jnp.int32, shape, 1)
    groups = columns // 8
    live = []
    for g in range(groups):
        unit = jnp.where(lane == row + (columns + 8 * g), 1.0, 0.0)
        live.append(jnp.concatenate([gram[8 * g:8 * g + 8, :], unit[:, columns:]], axis=1))
    done = []
    for g in range(groups):
        cols = [[jnp.broadcast_to(part[:, 8 * g + j:8 * g + j + 1], shape) for part in live] for j in range(8)]
        pivots = jnp.ones(shape, jnp.float32)
        for j in range(8):
            pivot = jnp.broadcast_to(cols[j][0][j:j+1], shape)
            pivots = jnp.where(row == j, pivot, pivots)
            inverse = 1.0 / pivot
            ratios = [part * inverse for part in cols[j]]
            ratios[0] = jnp.where(row > j, ratios[0], 0.0)
            for i in range(j + 1, 8):
                pick = jnp.broadcast_to(cols[i][0][j:j+1], shape)
                cols[i] = [part - ratio * pick for part, ratio in zip(cols[i], ratios)]
            pick = jnp.broadcast_to(live[0][j:j+1], shape)
            live = [part - ratio * pick for part, ratio in zip(live, ratios)]
        done.append(live[0] * lax.rsqrt(pivots))
        live = live[1:]
    whole = jnp.concatenate(done, axis=0)
    left, right = whole[:, :columns], whole[:, columns:]
    on_or_above = lax.broadcasted_iota(jnp.int32, left.shape, 0) <= lax.broadcasted_iota(jnp.int32, left.shape, 1)
    factor[...] = jnp.where(on_or_above, left, 0.0) * (1.0 / scale)
    weight = right * scale
    high = weight.astype(jnp.bfloat16)
    low = (weight - high.astype(jnp.float32)).astype(jnp.bfloat16)
    stacked = jnp.concatenate([high, high, low], axis=1)
    values = jnp.concatenate([split[...], split[:columns]], axis=0)
    basis[...] = jnp.dot(stacked, values, preferred_element_type=jnp.float32)


def in_vmem():
    return pl.BlockSpec(memory_space=pltpu.VMEM)


def in_smem():
    return pl.BlockSpec(memory_space=pltpu.SMEM)


def sum_over_all(value):
    gx_count, gy_count = lax.axis_size("gx"), lax.axis_size("gy")
    total = gx_count * gy_count
    bits = [gy_count * 2**i for i in range(1, gx_count.bit_length() - 1)]
    bits = bits[:1] + [2**i for i in range(gy_count.bit_length() - 1)] + bits[1:]

    def from_other(mask):
        return lax.ppermute(value, ("gx", "gy"), [(i, i ^ mask) for i in range(total)])

    value = value + from_other(gy_count)
    while bits:
        taken, bits = bits[:2], bits[2:]
        near = value + from_other(taken[0])
        if len(taken) == 2:
            near = near + (from_other(taken[1]) + from_other(taken[0] ^ taken[1]))
        value = near
    return value


def shards(near_tiles, block, adjacency):
    tiles_dev, blocks = adjacency.shape[2:]
    width = near_tiles.shape[4]
    rows, columns = block.shape[2:]
    gx_count, gy_count = lax.axis_size("gx"), lax.axis_size("gy")
    scale = float(rows * gx_count * gy_count) ** 0.5

    beside = pair_swap(block, "gy")
    two_off = two_back(block, "gy")
    outer = between_pairs(block, "gx")
    core = pair_swap(block, "gx")

    count = tiles_dev * blocks
    links = adjacency[0, 0].reshape(1, -1)
    near = near_tiles.reshape(count, width, width)
    acc_shape = jax.ShapeDtypeStruct((tiles_dev, width, columns), jnp.float32)
    flat = lambda value: value[0, 0].T

    def tile_rows(sources):
        return pltpu.VMEM((sources * tiles_dev + 1, columns, width), jnp.bfloat16)

    def params(limit=VMEM_LIMIT):
        return dict(
            compiler_params=pltpu.CompilerParams(vmem_limit_bytes=limit),
        )

    acc, work = pl.pallas_call(
        functools.partial(own_kernel, gy_count),
        out_shape=(acc_shape, jax.ShapeDtypeStruct((PARTS * LIST_ROWS + 2, 128), jnp.int32)),
        in_specs=[in_vmem(), pl.BlockSpec(memory_space=pltpu.HBM), in_vmem()],
        out_specs=(in_vmem(), in_vmem()),
        scratch_shapes=[
            tile_rows(1),
            pltpu.VMEM((EARLY * UNROLL, width, width), near.dtype),
            pltpu.SMEM((PARTS * LIST_ROWS + 2, 128), jnp.int32),
            pltpu.SemaphoreType.DMA((EARLY,)),
            pltpu.SemaphoreType.DMA,
        ],
        name="own_rows", **params(46 * 2**20),
    )(links, near, flat(block))

    def add(part, acc, *sources):
        return pl.pallas_call(
            functools.partial(middle_kernel, part), out_shape=acc_shape, out_specs=in_vmem(),
            in_specs=[in_smem()] + [in_vmem()] * (2 + len(sources)), scratch_shapes=[tile_rows(len(sources))],
            name=f"rows_{part}", input_output_aliases={2 + len(sources): 0}, **params(),
        )(work, near, *(flat(source) for source in sources), acc)

    beside, two_off, outer, core, acc = lax.optimization_barrier((beside, two_off, outer, core, acc))
    beyond = pair_swap(two_off, "gy")
    beside_outer = between_pairs(beside, "gx")
    beyond_outer = across_both(beside)
    beside_core = pair_swap(beside, "gx")
    near, acc = pl.pallas_call(
        loading_kernel,
        out_shape=(pltpu.VMEM(near.shape, near.dtype), acc_shape),
        in_specs=[in_smem(), pl.BlockSpec(memory_space=pltpu.HBM)] + [in_vmem()] * 6,
        out_specs=(in_vmem(), in_vmem()),
        scratch_shapes=[tile_rows(4), tile_rows(1), pltpu.SemaphoreType.DMA((CHUNKS,))],
        name="rows_1", input_output_aliases={7: 1}, **params(24 * 2**20),
    )(work, near, *(flat(source) for source in (block, core, outer, beside, beside_core)), acc)
    beyond, beside_outer, beyond_outer, acc = lax.optimization_barrier((beyond, beside_outer, beyond_outer, acc))
    beyond_core = pair_swap(beyond, "gx")
    acc = add(2, acc, beside_outer, beyond, beyond_outer)
    split, gram = pl.pallas_call(
        last_kernel,
        out_shape=(
            jax.ShapeDtypeStruct((2 * columns, rows), jnp.bfloat16),
            jax.ShapeDtypeStruct((columns, columns), jnp.float32),
        ),
        in_specs=[in_smem()] + [in_vmem()] * 3, out_specs=(in_vmem(), in_vmem()),
        scratch_shapes=[tile_rows(1), pltpu.VMEM(acc_shape.shape, jnp.float32)], name="rows_3_and_gram", **params(),
    )(work, near, flat(beyond_core), acc)

    gram = sum_over_all(gram)
    basis, factor = pl.pallas_call(
        functools.partial(finish_kernel, scale),
        out_shape=(
            jax.ShapeDtypeStruct((columns, rows), jnp.float32),
            jax.ShapeDtypeStruct((columns, columns), jnp.float32),
        ),
        in_specs=[in_vmem()] * 2, out_specs=(in_vmem(), in_vmem()), name="orthonormalize", **params(),
    )(gram, split)
    return basis.T.reshape(1, 1, rows, columns), factor


def solution(mesh):
    in_specs = (
        P("gx", "gy", None, None, None, None),
        P("gx", "gy", None, None),
        P("gx", "gy", None, None),
    )
    out_specs = (P("gx", "gy", None, None), P())
    return jax.shard_map(shards, mesh=mesh, in_specs=in_specs, out_specs=out_specs, check_vma=False)
```

```python
import functools

import jax
import jax.numpy as jnp
from jax import lax
from jax.experimental import pallas as pl
from jax.experimental.pallas import tpu as pltpu
from jax.sharding import PartitionSpec as P

UNROLL = 32
PARTS = 3
HALVES = 2
CHUNKS = 4
LIST_ROWS = 3
LINES = PARTS * HALVES * LIST_ROWS + 6
PART_OF = (0, 0, 0, 0, 0, 2, 1, 2, 1)
SLOT_OF = (0, 1, 2, 3, 4, 0, 0, 1, 1)
ROW_BY_ROW = (((1,), (1,)), ((), ()))
VMEM_LIMIT = 8 * 2**20


def pair_swap(value, axis):
    size = lax.axis_size(axis)
    return lax.ppermute(value, axis, [(i, i ^ 1) for i in range(size)])


def between_pairs(value, axis):
    return lax.ppermute(value, axis, outside(lax.axis_size(axis)))


def outside(size):
    return [(i, i + 1) for i in range(1, size - 1, 2)] + [(i + 1, i) for i in range(1, size - 1, 2)]


def across_both(value):
    gx_count, gy_count = lax.axis_size("gx"), lax.axis_size("gy")
    pairs = [
        (from_x * gy_count + (from_y ^ 1), to_x * gy_count + to_y)
        for from_x, to_x in outside(gx_count)
        for from_y, to_y in outside(gy_count)
    ]
    return lax.ppermute(value, ("gx", "gy"), pairs)


def two_back(value, axis):
    size = lax.axis_size(axis)
    pairs = [(i, i - 2) for i in range(2, size, 2)]
    pairs += [(i, i + 2) for i in range(1, size - 2, 2)]
    return lax.ppermute(value, axis, pairs)


def exact_log2(value):
    assert value & (value - 1) == 0
    return value.bit_length() - 1


def look_up(table, index):
    packed = sum(value << (3 * place) for place, value in enumerate(table))
    return lax.shift_right_logical(jnp.full(index.shape, packed, jnp.int32), 3 * index) & 7


def build_lists(links, work, tiles_dev, blocks, gy_count):
    own_x, own_y = lax.axis_index("gx"), lax.axis_index("gy")
    count = links.shape[0] * links.shape[2]
    tile_bits, gy_bits = exact_log2(tiles_dev), exact_log2(gy_count)
    link = jnp.concatenate([links[block] for block in range(blocks)], axis=1)
    order = lax.broadcasted_iota(jnp.int32, link.shape, 1)
    tile = order & (tiles_dev - 1)
    place = tile * blocks + lax.shift_right_logical(order, tile_bits)
    owner = lax.shift_right_logical(link, tile_bits)
    owner_x, owner_y = lax.shift_right_logical(owner, gy_bits), owner & (gy_count - 1)
    across = jnp.where(owner_x == own_x, 0, jnp.where(owner_x == (own_x ^ 1), 1, 2))
    own_row, beside = owner_y == own_y, owner_y == (own_y ^ 1)
    kind = across + jnp.where(own_row, 0, jnp.where(beside, 3, 6))
    part, slot = look_up(PART_OF, kind), look_up(SLOT_OF, kind)
    half = lax.shift_right_logical(tile, tile_bits - 1)
    code = (place - half * (count // HALVES)) * 512 + slot * tiles_dev + (link & (tiles_dev - 1)) + 1

    def ones_where(hit):
        return jnp.where(hit, 1.0, 0.0).astype(jnp.bfloat16)

    def iota(shape, dim):
        return lax.broadcasted_iota(jnp.int32, shape, dim)

    def dot(left, right):
        return jnp.dot(left, right, preferred_element_type=jnp.float32)

    def row_dot(left, right):
        return lax.dot_general(left, right, ROW_BY_ROW, preferred_element_type=jnp.float32)

    def to_even(length):
        return ((length.astype(jnp.int32) + 1) & -2).astype(jnp.float32).astype(jnp.bfloat16)

    groups, lines = PARTS * tiles_dev, LINES
    group = part * tiles_dev + tile
    in_group = iota((groups, count), 0) == group
    members = ones_where(in_group)
    before = dot(members, ones_where(iota((count, count), 0) < iota((count, count), 1)))
    lengths = dot(members, jnp.ones((count, 128), jnp.bfloat16))
    first, second = iota((groups, groups), 0), iota((groups, groups), 1)
    half_bits = tile_bits - 1
    same_list = lax.shift_right_logical(first, half_bits) == lax.shift_right_logical(second, half_bits)
    starts = dot(ones_where(same_list & (second < first)), to_even(lengths))
    rank = jnp.sum(jnp.where(in_group, before + starts[:, :1], 0.0), axis=0, keepdims=True).astype(jnp.int32)
    row = (part * HALVES + half) * LIST_ROWS + lax.shift_right_logical(rank, 7)
    column_hits = ones_where(iota((128, count), 0) == (rank & 127))
    row_hits = iota((lines, count), 0) == row
    listed = jnp.zeros((lines, 128), jnp.float32)
    for shift in (16, 8, 0):
        digit = (lax.shift_right_logical(code, shift) & 255).astype(jnp.float32)
        listed = listed * 256.0 + row_dot(jnp.where(row_hits, digit, 0.0).astype(jnp.bfloat16), column_hits)
    by_group = to_even(row_dot(jnp.ones((lines, count), jnp.bfloat16), members))
    of_list = iota((128, groups), 0) == lax.shift_right_logical(iota((128, groups), 1), half_bits)
    totals = row_dot(by_group, ones_where(of_list))
    work[...] = jnp.where(iota((lines, 128), 0) == lines - 1, totals, listed).astype(jnp.int32)


def lay_out(sources, rows, tiles_dev):
    width = rows.shape[-1]
    rows[0] = jnp.zeros(rows.shape[1:], rows.dtype)
    for slot, source in enumerate(sources):
        for tile in range(tiles_dev):
            rows[1 + slot * tiles_dev + tile] = source[:, tile * width:(tile + 1) * width]


def batches(part, half, work):
    return lax.div(work[LINES - 1, part * HALVES + half] + (UNROLL - 1), UNROLL)


def products_of(part, half, work, index, near, acc, rows):
    tiles_half = acc.shape[0] // HALVES
    blocks = near.shape[0] // tiles_half
    groups = 128 // UNROLL
    line = (part * HALVES + half) * LIST_ROWS + lax.div(index, groups)
    begin = lax.rem(index, groups) * UNROLL
    products = []
    for lane in range(0, UNROLL, 2):
        codes = [work[line, begin + lane + i] for i in range(2)]
        entries = [lax.shift_right_logical(code, 9) for code in codes]
        left = jnp.concatenate([near[entry] for entry in entries], axis=1)
        right = jnp.concatenate([rows[code & 511] for code in codes], axis=1)
        product = lax.dot_general(left, right, ROW_BY_ROW, preferred_element_type=jnp.float32)
        products.append((lax.div(entries[0], blocks) + half * tiles_half, product))
    return products


def add_all(products, acc):
    for target, product in products:
        acc[target] += product


def add_both(part, work, nears, acc, rows):
    def step(index, carry):
        products = []
        for half, near in enumerate(nears):
            products += products_of(part, half, work, index, near, acc, rows)
        add_all(products, acc)
        return carry

    longest = jnp.maximum(*(batches(part, half, work) for half in range(HALVES)))
    lax.fori_loop(0, longest, step, 0)


def loads_of(half, near_hbm, near, sems):
    chunks = sems.shape[1]
    length = near.shape[0] // chunks
    return [
        pltpu.make_async_copy(
            near_hbm.at[pl.ds(half * near.shape[0] + chunk * length, length)],
            near.at[pl.ds(chunk * length, length)],
            sems.at[half, chunk],
        )
        for chunk in range(chunks)
    ]


def load_kernel(tiles_dev, gy_count, links, near_hbm, near_0, near_1, work, sems):
    loads = [load for half, near in enumerate((near_0, near_1)) for load in loads_of(half, near_hbm, near, sems)]
    for load in loads:
        load.start()
    build_lists(links, work, tiles_dev, near_hbm.shape[0] // tiles_dev, gy_count)
    for load in loads:
        load.wait()


def early_kernel(work_in, near_0, near_1, *refs):
    acc, rows, work, sem = refs[-4:]
    copy = pltpu.make_async_copy(work_in, work, sem)
    copy.start()
    lay_out(refs[:-4], rows, acc.shape[0])
    acc[...] = jnp.zeros(acc.shape, acc.dtype)
    copy.wait()
    add_both(0, work, (near_0, near_1), acc, rows)


def next_kernel(work_in, near_0, near_1, *refs):
    acc, rows, work, sem = refs[-4:]
    copy = pltpu.make_async_copy(work_in, work, sem)
    copy.start()
    lay_out(refs[:-5], rows, acc.shape[0])
    copy.wait()
    add_both(1, work, (near_0, near_1), acc, rows)


def last_kernel(work_in, near_0, near_1, outer, core, acc_in, split, gram, acc, rows, work, sem):
    tiles_dev, width, columns = acc.shape
    copy = pltpu.make_async_copy(work_in, work, sem)
    copy.start()
    lay_out((outer, core), rows, tiles_dev)
    copy.wait()
    add_both(2, work, (near_0, near_1), acc, rows)
    for tile in range(tiles_dev):
        image = acc[tile].T
        high = image.astype(jnp.bfloat16)
        low = (image - high.astype(jnp.float32)).astype(jnp.bfloat16)
        split[:, tile * width:(tile + 1) * width] = jnp.concatenate([high, low], axis=0)
    both = split[...]
    full = lax.dot_general(both, both, ROW_BY_ROW, preferred_element_type=jnp.float32)
    top = full[:columns, :columns] + full[columns:, columns:]
    side = full[:columns, columns:] + full[columns:, :columns]
    total = top + side
    gram[...] = jnp.concatenate([total[:columns // 2], total[columns // 2:]], axis=1)


def finish_kernel(scale, gram, split, basis, factor):
    columns = 2 * gram.shape[0]
    shape = (8, 2 * columns)
    row = lax.broadcasted_iota(jnp.int32, shape, 0)
    lane = lax.broadcasted_iota(jnp.int32, shape, 1)
    groups = columns // 8
    live = []
    for g in range(groups):
        unit = jnp.where(lane == row + (columns + 8 * g), 1.0, 0.0)
        begin, side = 8 * g % (columns // 2), 8 * g // (columns // 2) * columns
        live.append(jnp.concatenate([gram[begin:begin + 8, side:side + columns], unit[:, columns:]], axis=1))
    done = []
    for g in range(groups):
        cols = [[jnp.broadcast_to(part[:, 8 * g + j:8 * g + j + 1], shape) for part in live] for j in range(8)]
        pivots = jnp.ones(shape, jnp.float32)
        for j in range(8):
            pivot = jnp.broadcast_to(cols[j][0][j:j+1], shape)
            pivots = jnp.where(row == j, pivot, pivots)
            inverse = 1.0 / pivot
            ratios = [part * inverse for part in cols[j]]
            ratios[0] = jnp.where(row > j, ratios[0], 0.0)
            for i in range(j + 1, 8):
                pick = jnp.broadcast_to(cols[i][0][j:j+1], shape)
                cols[i] = [part - ratio * pick for part, ratio in zip(cols[i], ratios)]
            pick = jnp.broadcast_to(live[0][j:j+1], shape)
            live = [part - ratio * pick for part, ratio in zip(live, ratios)]
        done.append(live[0] * lax.rsqrt(pivots))
        live = live[1:]
    whole = jnp.concatenate(done, axis=0)
    left, right = whole[:, :columns], whole[:, columns:]
    on_or_above = lax.broadcasted_iota(jnp.int32, left.shape, 0) <= lax.broadcasted_iota(jnp.int32, left.shape, 1)
    factor[...] = jnp.where(on_or_above, left, 0.0) * (1.0 / scale)
    weight = right * scale
    high = weight.astype(jnp.bfloat16)
    low = (weight - high.astype(jnp.float32)).astype(jnp.bfloat16)
    stacked = jnp.concatenate([high, high, low], axis=1)
    values = jnp.concatenate([split[...], split[:columns]], axis=0)
    basis[...] = jnp.dot(stacked, values, preferred_element_type=jnp.float32)


def in_vmem():
    return pl.BlockSpec(memory_space=pltpu.VMEM)


def sum_over_all(value):
    gx_count, gy_count = lax.axis_size("gx"), lax.axis_size("gy")
    total = gx_count * gy_count
    bits = [gy_count * 2**i for i in range(1, gx_count.bit_length() - 1)]
    bits = bits[:1] + [2**i for i in range(gy_count.bit_length() - 1)] + bits[1:]

    def from_other(mask):
        return lax.ppermute(value, ("gx", "gy"), [(i, i ^ mask) for i in range(total)])

    value = value + from_other(gy_count)
    while bits:
        taken, bits = bits[:2], bits[2:]
        near = value + from_other(taken[0])
        if len(taken) == 2:
            near = near + (from_other(taken[1]) + from_other(taken[0] ^ taken[1]))
        value = near
    return value


def shards(near_tiles, block, adjacency):
    tiles_dev, blocks = adjacency.shape[2:]
    width = near_tiles.shape[4]
    rows, columns = block.shape[2:]
    gx_count, gy_count = lax.axis_size("gx"), lax.axis_size("gy")
    scale = float(rows * gx_count * gy_count) ** 0.5

    beside = pair_swap(block, "gy")
    two_off = two_back(block, "gy")
    outer = between_pairs(block, "gx")
    core = pair_swap(block, "gx")

    count = tiles_dev * blocks
    links = adjacency[0, 0].T.reshape(blocks, 1, tiles_dev)
    near = near_tiles.reshape(count, width, width)
    acc_shape = jax.ShapeDtypeStruct((tiles_dev, width, columns), jnp.float32)
    flat = lambda value: value[0, 0].T

    def tile_rows(sources):
        return pltpu.VMEM((sources * tiles_dev + 1, columns, width), jnp.bfloat16)

    def params(limit=VMEM_LIMIT):
        return dict(
            compiler_params=pltpu.CompilerParams(vmem_limit_bytes=limit),
        )

    work_scratch = [pltpu.SMEM((LINES, 128), jnp.int32), pltpu.SemaphoreType.DMA]
    near_half = pltpu.VMEM((count // HALVES, width, width), near.dtype)
    near_0, near_1, work = pl.pallas_call(
        functools.partial(load_kernel, tiles_dev, gy_count),
        out_shape=(near_half, near_half, jax.ShapeDtypeStruct((LINES, 128), jnp.int32)),
        in_specs=[in_vmem(), pl.BlockSpec(memory_space=pltpu.HBM)], out_specs=(in_vmem(),) * 3,
        scratch_shapes=[pltpu.SemaphoreType.DMA((HALVES, CHUNKS))], name="load", **params(24 * 2**20),
    )(links, near)

    beside, two_off, work = lax.optimization_barrier((beside, two_off, work))
    beyond = pair_swap(two_off, "gy")
    beside_outer = between_pairs(beside, "gx")
    beyond_outer = across_both(beside)
    beside_core = pair_swap(beside, "gx")
    sources = (block, core, outer, beside, beside_core)
    acc = pl.pallas_call(
        early_kernel, out_shape=acc_shape, in_specs=[in_vmem()] * 8, out_specs=in_vmem(),
        scratch_shapes=[tile_rows(5)] + work_scratch, name="early_rows", **params(),
    )(work, near_0, near_1, *(flat(source) for source in sources))

    beyond, beyond_outer, acc = lax.optimization_barrier((beyond, beyond_outer, acc))
    beyond_core = pair_swap(beyond, "gx")
    acc = pl.pallas_call(
        next_kernel, out_shape=acc_shape, in_specs=[in_vmem()] * 6, out_specs=in_vmem(),
        scratch_shapes=[tile_rows(2)] + work_scratch, name="next_rows", input_output_aliases={5: 0}, **params(),
    )(work, near_0, near_1, flat(beyond), flat(beyond_outer), acc)

    beside_outer, beyond_core, acc = lax.optimization_barrier((beside_outer, beyond_core, acc))
    split, gram, _ = pl.pallas_call(
        last_kernel,
        out_shape=(
            jax.ShapeDtypeStruct((2 * columns, rows), jnp.bfloat16),
            jax.ShapeDtypeStruct((columns // 2, 2 * columns), jnp.float32),
            acc_shape,
        ),
        in_specs=[in_vmem()] * 6, out_specs=(in_vmem(),) * 3,
        scratch_shapes=[tile_rows(2)] + work_scratch, name="last_rows_and_gram", input_output_aliases={5: 2}, **params(),
    )(work, near_0, near_1, flat(beside_outer), flat(beyond_core), acc)

    gram = sum_over_all(gram)
    basis, factor = pl.pallas_call(
        functools.partial(finish_kernel, scale),
        out_shape=(
            jax.ShapeDtypeStruct((columns, rows), jnp.float32),
            jax.ShapeDtypeStruct((columns, columns), jnp.float32),
        ),
        in_specs=[in_vmem()] * 2, out_specs=(in_vmem(), in_vmem()), name="orthonormalize", **params(),
    )(gram, split)
    return basis.T.reshape(1, 1, rows, columns), factor


def solution(mesh):
    in_specs = (
        P("gx", "gy", None, None, None, None),
        P("gx", "gy", None, None),
        P("gx", "gy", None, None),
    )
    out_specs = (P("gx", "gy", None, None), P())
    return jax.shard_map(shards, mesh=mesh, in_specs=in_specs, out_specs=out_specs, check_vma=False)
```

```python
import functools

import jax
import jax.numpy as jnp
from jax import lax
from jax.experimental import pallas as pl
from jax.experimental.pallas import tpu as pltpu
from jax.sharding import PartitionSpec as P

UNROLL = 32
PARTS = 3
HALVES = 2
CHUNKS = 4
AHEAD = 2
LIST_ROWS = 3
LINES = PARTS * HALVES * LIST_ROWS + 6
PART_OF = (0, 0, 0, 0, 0, 2, 1, 2, 1)
SLOT_OF = (0, 1, 2, 3, 4, 0, 0, 1, 1)
ROW_BY_ROW = (((1,), (1,)), ((), ()))
VMEM_LIMIT = 8 * 2**20


def pair_swap(value, axis):
    size = lax.axis_size(axis)
    return lax.ppermute(value, axis, [(i, i ^ 1) for i in range(size)])


def between_pairs(value, axis):
    return lax.ppermute(value, axis, outside(lax.axis_size(axis)))


def outside(size):
    return [(i, i + 1) for i in range(1, size - 1, 2)] + [(i + 1, i) for i in range(1, size - 1, 2)]


def pass_on(value, axis):
    pairs = [(sender ^ 1, receiver) for sender, receiver in outside(lax.axis_size(axis))]
    return lax.ppermute(value, axis, pairs)


def swap_of_outer(value):
    gx_count, gy_count = lax.axis_size("gx"), lax.axis_size("gy")
    pairs = [(x * gy_count + y, x * gy_count + (y ^ 1)) for x, _ in outside(gx_count) for y in range(gy_count)]
    return lax.ppermute(value, ("gx", "gy"), pairs)


def to_mate_of_outside(value):
    gx_count, gy_count = lax.axis_size("gx"), lax.axis_size("gy")
    pairs = [
        (x * gy_count + sender, x * gy_count + (receiver ^ 1))
        for x, _ in outside(gx_count)
        for sender, receiver in outside(gy_count)
    ]
    return lax.ppermute(value, ("gx", "gy"), pairs)


def from_mate_across(value):
    gx_count, gy_count = lax.axis_size("gx"), lax.axis_size("gy")
    pairs = [
        (from_x * gy_count + (receiver ^ 1), to_x * gy_count + receiver)
        for from_x, to_x in outside(gx_count)
        for _, receiver in outside(gy_count)
    ]
    return lax.ppermute(value, ("gx", "gy"), pairs)


def exact_log2(value):
    assert value & (value - 1) == 0
    return value.bit_length() - 1


def look_up(table, index):
    packed = sum(value << (3 * place) for place, value in enumerate(table))
    return lax.shift_right_logical(jnp.full(index.shape, packed, jnp.int32), 3 * index) & 7


def build_lists(links, work, tiles_dev, blocks, gy_count):
    own_x, own_y = lax.axis_index("gx"), lax.axis_index("gy")
    count = links.shape[0] * links.shape[2]
    tile_bits, gy_bits = exact_log2(tiles_dev), exact_log2(gy_count)
    link = jnp.concatenate([links[block] for block in range(blocks)], axis=1)
    order = lax.broadcasted_iota(jnp.int32, link.shape, 1)
    tile = order & (tiles_dev - 1)
    place = tile * blocks + lax.shift_right_logical(order, tile_bits)
    owner = lax.shift_right_logical(link, tile_bits)
    owner_x, owner_y = lax.shift_right_logical(owner, gy_bits), owner & (gy_count - 1)
    across = jnp.where(owner_x == own_x, 0, jnp.where(owner_x == (own_x ^ 1), 1, 2))
    own_row, beside = owner_y == own_y, owner_y == (own_y ^ 1)
    kind = across + jnp.where(own_row, 0, jnp.where(beside, 3, 6))
    part, slot = look_up(PART_OF, kind), look_up(SLOT_OF, kind)
    half = lax.shift_right_logical(tile, tile_bits - 1)
    code = (place - half * (count // HALVES)) * 512 + slot * tiles_dev + (link & (tiles_dev - 1)) + 1

    def ones_where(hit):
        return jnp.where(hit, 1.0, 0.0).astype(jnp.bfloat16)

    def iota(shape, dim):
        return lax.broadcasted_iota(jnp.int32, shape, dim)

    def dot(left, right):
        return jnp.dot(left, right, preferred_element_type=jnp.float32)

    def row_dot(left, right):
        return lax.dot_general(left, right, ROW_BY_ROW, preferred_element_type=jnp.float32)

    def to_even(length):
        return ((length.astype(jnp.int32) + 1) & -2).astype(jnp.float32).astype(jnp.bfloat16)

    groups, lines = PARTS * tiles_dev, LINES
    group = part * tiles_dev + tile
    in_group = iota((groups, count), 0) == group
    members = ones_where(in_group)
    before = dot(members, ones_where(iota((count, count), 0) < iota((count, count), 1)))
    lengths = dot(members, jnp.ones((count, 128), jnp.bfloat16))
    first, second = iota((groups, groups), 0), iota((groups, groups), 1)
    half_bits = tile_bits - 1
    same_list = lax.shift_right_logical(first, half_bits) == lax.shift_right_logical(second, half_bits)
    starts = dot(ones_where(same_list & (second < first)), to_even(lengths))
    rank = jnp.sum(jnp.where(in_group, before + starts[:, :1], 0.0), axis=0, keepdims=True).astype(jnp.int32)
    row = (part * HALVES + half) * LIST_ROWS + lax.shift_right_logical(rank, 7)
    column_hits = ones_where(iota((128, count), 0) == (rank & 127))
    row_hits = iota((lines, count), 0) == row
    listed = jnp.zeros((lines, 128), jnp.float32)
    for shift in (16, 8, 0):
        digit = (lax.shift_right_logical(code, shift) & 255).astype(jnp.float32)
        listed = listed * 256.0 + row_dot(jnp.where(row_hits, digit, 0.0).astype(jnp.bfloat16), column_hits)
    by_group = to_even(row_dot(jnp.ones((lines, count), jnp.bfloat16), members))
    of_list = iota((128, groups), 0) == lax.shift_right_logical(iota((128, groups), 1), half_bits)
    totals = row_dot(by_group, ones_where(of_list))
    work[...] = jnp.where(iota((lines, 128), 0) == lines - 1, totals, listed).astype(jnp.int32)


def lay_out(sources, rows, tiles_dev):
    width = rows.shape[-1]
    rows[0] = jnp.zeros(rows.shape[1:], rows.dtype)
    for slot, source in enumerate(sources):
        for tile in range(tiles_dev):
            rows[1 + slot * tiles_dev + tile] = source[:, tile * width:(tile + 1) * width]


def batches(part, half, work):
    return lax.div(work[LINES - 1, part * HALVES + half] + (UNROLL - 1), UNROLL)


def products_of(part, half, work, index, near, acc, rows):
    tiles_half = acc.shape[0] // HALVES
    blocks = near.shape[0] // tiles_half
    groups = 128 // UNROLL
    line = (part * HALVES + half) * LIST_ROWS + lax.div(index, groups)
    begin = lax.rem(index, groups) * UNROLL
    products = []
    for lane in range(0, UNROLL, 2):
        codes = [work[line, begin + lane + i] for i in range(2)]
        entries = [lax.shift_right_logical(code, 9) for code in codes]
        left = jnp.concatenate([near[entry] for entry in entries], axis=1)
        right = jnp.concatenate([rows[code & 511] for code in codes], axis=1)
        product = lax.dot_general(left, right, ROW_BY_ROW, preferred_element_type=jnp.float32)
        products.append((lax.div(entries[0], blocks) + half * tiles_half, product))
    return products


def add_all(products, acc):
    for target, product in products:
        acc[target] += product


def add_both(part, work, nears, acc, rows):
    def step(index, carry):
        products = []
        for half, near in enumerate(nears):
            products += products_of(part, half, work, index, near, acc, rows)
        add_all(products, acc)
        return carry

    longest = jnp.maximum(*(batches(part, half, work) for half in range(HALVES)))
    lax.fori_loop(0, longest, step, 0)


def loads_of(half, near_hbm, near, sems):
    length = near.shape[0] // CHUNKS
    return [
        pltpu.make_async_copy(
            near_hbm.at[pl.ds(half * near.shape[0] + chunk * length, length)],
            near.at[pl.ds(chunk * length, length)],
            sems.at[chunk],
        )
        for chunk in range(CHUNKS)
    ]


def load_kernel(tiles_dev, gy_count, links, near_hbm, near_0, near_1, work, sems):
    loads = loads_of(0, near_hbm, near_0, sems.at[0]) + loads_of(1, near_hbm, near_1, sems.at[1])[:AHEAD]
    for load in loads:
        load.start()
    build_lists(links, work, tiles_dev, near_hbm.shape[0] // tiles_dev, gy_count)
    for load in loads:
        load.wait()


def early_kernel(work_in, near_hbm, near_0, near_in, *refs):
    near_1, acc, rows, work, sem, sems = refs[-6:]
    loads = loads_of(1, near_hbm, near_1, sems)
    for load in loads[AHEAD:]:
        load.start()
    copy = pltpu.make_async_copy(work_in, work, sem)
    copy.start()
    lay_out(refs[:-6], rows, acc.shape[0])
    acc[...] = jnp.zeros(acc.shape, acc.dtype)
    copy.wait()
    length = near_1.shape[0] // CHUNKS
    count = batches(0, 1, work)

    def wait(chunk, carry):
        held = near_1.at[pl.ds(chunk * length, length)]
        pltpu.make_async_copy(near_hbm.at[pl.ds(chunk * length, length)], held, sems.at[chunk]).wait()
        return carry

    def step(index, there):
        groups = 128 // UNROLL
        last = work[LIST_ROWS + lax.div(index, groups), lax.rem(index, groups) * UNROLL + UNROLL - 2]
        needed = jnp.where(index >= count - 1, CHUNKS, lax.div(lax.shift_right_logical(last, 9), length) + 1)
        lax.fori_loop(there, needed, wait, 0)
        products = []
        for half, near in enumerate((near_0, near_1)):
            products += products_of(0, half, work, index, near, acc, rows)
        add_all(products, acc)
        return jnp.maximum(there, needed)

    there = lax.fori_loop(0, jnp.maximum(batches(0, 0, work), count), step, jnp.int32(AHEAD))
    lax.fori_loop(there, CHUNKS, wait, 0)


def next_kernel(work_in, near_0, near_1, *refs):
    acc, rows, work, sem = refs[-4:]
    copy = pltpu.make_async_copy(work_in, work, sem)
    copy.start()
    lay_out(refs[:-5], rows, acc.shape[0])
    copy.wait()
    add_both(1, work, (near_0, near_1), acc, rows)


def last_kernel(work_in, near_0, near_1, outer, core, acc_in, split, gram, acc, rows, work, sem):
    tiles_dev, width, columns = acc.shape
    copy = pltpu.make_async_copy(work_in, work, sem)
    copy.start()
    lay_out((outer, core), rows, tiles_dev)
    copy.wait()
    add_both(2, work, (near_0, near_1), acc, rows)
    for tile in range(tiles_dev):
        image = acc[tile].T
        high = image.astype(jnp.bfloat16)
        low = (image - high.astype(jnp.float32)).astype(jnp.bfloat16)
        split[:, tile * width:(tile + 1) * width] = jnp.concatenate([high, low], axis=0)
    both = split[...]
    full = lax.dot_general(both, both, ROW_BY_ROW, preferred_element_type=jnp.float32)
    top = full[:columns, :columns] + full[columns:, columns:]
    side = full[:columns, columns:] + full[columns:, :columns]
    total = top + side
    gram[...] = jnp.concatenate([total[:columns // 2], total[columns // 2:]], axis=1)


def finish_kernel(scale, gram, split, basis, factor):
    columns = 2 * gram.shape[0]
    shape = (8, 2 * columns)
    row = lax.broadcasted_iota(jnp.int32, shape, 0)
    lane = lax.broadcasted_iota(jnp.int32, shape, 1)
    groups = columns // 8
    live = []
    for g in range(groups):
        unit = jnp.where(lane == row + (columns + 8 * g), 1.0, 0.0)
        begin, side = 8 * g % (columns // 2), 8 * g // (columns // 2) * columns
        live.append(jnp.concatenate([gram[begin:begin + 8, side:side + columns], unit[:, columns:]], axis=1))
    done = []
    for g in range(groups):
        cols = [[jnp.broadcast_to(part[:, 8 * g + j:8 * g + j + 1], shape) for part in live] for j in range(8)]
        pivots = jnp.ones(shape, jnp.float32)
        for j in range(8):
            pivot = jnp.broadcast_to(cols[j][0][j:j+1], shape)
            pivots = jnp.where(row == j, pivot, pivots)
            inverse = 1.0 / pivot
            ratios = [part * inverse for part in cols[j]]
            ratios[0] = jnp.where(row > j, ratios[0], 0.0)
            for i in range(j + 1, 8):
                pick = jnp.broadcast_to(cols[i][0][j:j+1], shape)
                cols[i] = [part - ratio * pick for part, ratio in zip(cols[i], ratios)]
            pick = jnp.broadcast_to(live[0][j:j+1], shape)
            live = [part - ratio * pick for part, ratio in zip(live, ratios)]
        done.append(live[0] * lax.rsqrt(pivots))
        live = live[1:]
    whole = jnp.concatenate(done, axis=0)
    left, right = whole[:, :columns], whole[:, columns:]
    on_or_above = lax.broadcasted_iota(jnp.int32, left.shape, 0) <= lax.broadcasted_iota(jnp.int32, left.shape, 1)
    factor[...] = jnp.where(on_or_above, left, 0.0) * (1.0 / scale)
    weight = right * scale
    high = weight.astype(jnp.bfloat16)
    low = (weight - high.astype(jnp.float32)).astype(jnp.bfloat16)
    stacked = jnp.concatenate([high, high, low], axis=1)
    values = jnp.concatenate([split[...], split[:columns]], axis=0)
    basis[...] = jnp.dot(stacked, values, preferred_element_type=jnp.float32)


def in_vmem():
    return pl.BlockSpec(memory_space=pltpu.VMEM)


def sum_over_all(value):
    gx_count, gy_count = lax.axis_size("gx"), lax.axis_size("gy")
    total = gx_count * gy_count
    bits = [gy_count * 2**i for i in range(1, gx_count.bit_length() - 1)]
    bits = bits[:1] + [2**i for i in range(gy_count.bit_length() - 1)] + bits[1:]

    def from_other(mask):
        return lax.ppermute(value, ("gx", "gy"), [(i, i ^ mask) for i in range(total)])

    value = value + from_other(gy_count)
    while bits:
        taken, bits = bits[:2], bits[2:]
        near = value + from_other(taken[0])
        if len(taken) == 2:
            near = near + (from_other(taken[1]) + from_other(taken[0] ^ taken[1]))
        value = near
    return value


def shards(near_tiles, block, adjacency):
    tiles_dev, blocks = adjacency.shape[2:]
    width = near_tiles.shape[4]
    rows, columns = block.shape[2:]
    gx_count, gy_count = lax.axis_size("gx"), lax.axis_size("gy")
    scale = float(rows * gx_count * gy_count) ** 0.5

    beside = pair_swap(block, "gy")
    two_off = to_mate_of_outside(block)
    outer = between_pairs(block, "gx")
    core = pair_swap(block, "gx")

    count = tiles_dev * blocks
    links = adjacency[0, 0].T.reshape(blocks, 1, tiles_dev)
    near = near_tiles.reshape(count, width, width)
    acc_shape = jax.ShapeDtypeStruct((tiles_dev, width, columns), jnp.float32)
    flat = lambda value: value[0, 0].T

    def tile_rows(sources):
        return pltpu.VMEM((sources * tiles_dev + 1, columns, width), jnp.bfloat16)

    def params(limit=VMEM_LIMIT):
        return dict(
            compiler_params=pltpu.CompilerParams(vmem_limit_bytes=limit),
        )

    work_scratch = [pltpu.SMEM((LINES, 128), jnp.int32), pltpu.SemaphoreType.DMA]
    near_half = pltpu.VMEM((count // HALVES, width, width), near.dtype)
    near_0, near_1, work = pl.pallas_call(
        functools.partial(load_kernel, tiles_dev, gy_count),
        out_shape=(near_half, near_half, jax.ShapeDtypeStruct((LINES, 128), jnp.int32)),
        in_specs=[in_vmem(), pl.BlockSpec(memory_space=pltpu.HBM)], out_specs=(in_vmem(),) * 3,
        scratch_shapes=[pltpu.SemaphoreType.DMA((HALVES, CHUNKS))], name="load", **params(24 * 2**20),
    )(links, near)

    beside, two_off, work = lax.optimization_barrier((beside, two_off, work))
    beyond = pass_on(beside, "gy")
    beside_outer = swap_of_outer(outer)
    beyond_outer = from_mate_across(two_off)
    beside_core = pair_swap(beside, "gx")
    sources = (block, core, outer, beside, beside_core)
    near_1, acc = pl.pallas_call(
        early_kernel, out_shape=(near_half, acc_shape),
        in_specs=[in_vmem(), pl.BlockSpec(memory_space=pltpu.HBM)] + [in_vmem()] * 7, out_specs=(in_vmem(),) * 2,
        scratch_shapes=[tile_rows(5)] + work_scratch + [pltpu.SemaphoreType.DMA((CHUNKS,))],
        name="early_rows", input_output_aliases={3: 0}, **params(24 * 2**20),
    )(work, near, near_0, near_1, *(flat(source) for source in sources))

    beyond, beyond_outer, acc = lax.optimization_barrier((beyond, beyond_outer, acc))
    beyond_core = pair_swap(beyond, "gx")
    acc = pl.pallas_call(
        next_kernel, out_shape=acc_shape, in_specs=[in_vmem()] * 6, out_specs=in_vmem(),
        scratch_shapes=[tile_rows(2)] + work_scratch, name="next_rows", input_output_aliases={5: 0}, **params(),
    )(work, near_0, near_1, flat(beyond), flat(beyond_outer), acc)

    beside_outer, beyond_core, acc = lax.optimization_barrier((beside_outer, beyond_core, acc))
    split, gram, _ = pl.pallas_call(
        last_kernel,
        out_shape=(
            jax.ShapeDtypeStruct((2 * columns, rows), jnp.bfloat16),
            jax.ShapeDtypeStruct((columns // 2, 2 * columns), jnp.float32),
            acc_shape,
        ),
        in_specs=[in_vmem()] * 6, out_specs=(in_vmem(),) * 3,
        scratch_shapes=[tile_rows(2)] + work_scratch, name="last_rows_and_gram", input_output_aliases={5: 2}, **params(),
    )(work, near_0, near_1, flat(beside_outer), flat(beyond_core), acc)

    gram = sum_over_all(gram)
    basis, factor = pl.pallas_call(
        functools.partial(finish_kernel, scale),
        out_shape=(
            jax.ShapeDtypeStruct((columns, rows), jnp.float32),
            jax.ShapeDtypeStruct((columns, columns), jnp.float32),
        ),
        in_specs=[in_vmem()] * 2, out_specs=(in_vmem(), in_vmem()), name="orthonormalize", **params(),
    )(gram, split)
    return basis.T.reshape(1, 1, rows, columns), factor


def solution(mesh):
    in_specs = (
        P("gx", "gy", None, None, None, None),
        P("gx", "gy", None, None),
        P("gx", "gy", None, None),
    )
    out_specs = (P("gx", "gy", None, None), P())
    return jax.shard_map(shards, mesh=mesh, in_specs=in_specs, out_specs=out_specs, check_vma=False)
```

```python
import functools

import jax
import jax.numpy as jnp
from jax import lax
from jax.experimental import pallas as pl
from jax.experimental.pallas import tpu as pltpu
from jax.sharding import PartitionSpec as P

UNROLL = 32
PARTS = 3
HALVES = 2
CHUNKS = 4
AHEAD = 2
LIST_ROWS = 3
LINES = PARTS * HALVES * LIST_ROWS + 6
PART_OF = (0, 0, 0, 0, 0, 2, 1, 2, 1)
SLOT_OF = (0, 1, 2, 3, 4, 0, 0, 1, 1)
ROW_BY_ROW = (((1,), (1,)), ((), ()))
VMEM_LIMIT = 8 * 2**20


def pair_swap(value, axis):
    size = lax.axis_size(axis)
    return lax.ppermute(value, axis, [(i, i ^ 1) for i in range(size)])


def between_pairs(value, axis):
    return lax.ppermute(value, axis, outside(lax.axis_size(axis)))


def outside(size):
    return [(i, i + 1) for i in range(1, size - 1, 2)] + [(i + 1, i) for i in range(1, size - 1, 2)]


def pass_on(value, axis):
    pairs = [(sender ^ 1, receiver) for sender, receiver in outside(lax.axis_size(axis))]
    return lax.ppermute(value, axis, pairs)


def swap_of_outer(value):
    gx_count, gy_count = lax.axis_size("gx"), lax.axis_size("gy")
    pairs = [(x * gy_count + y, x * gy_count + (y ^ 1)) for x, _ in outside(gx_count) for y in range(gy_count)]
    return lax.ppermute(value, ("gx", "gy"), pairs)


def to_mate_of_outside(value):
    gx_count, gy_count = lax.axis_size("gx"), lax.axis_size("gy")
    pairs = [
        (x * gy_count + sender, x * gy_count + (receiver ^ 1))
        for x, _ in outside(gx_count)
        for sender, receiver in outside(gy_count)
    ]
    return lax.ppermute(value, ("gx", "gy"), pairs)


def from_mate_across(value):
    gx_count, gy_count = lax.axis_size("gx"), lax.axis_size("gy")
    pairs = [
        (from_x * gy_count + (receiver ^ 1), to_x * gy_count + receiver)
        for from_x, to_x in outside(gx_count)
        for _, receiver in outside(gy_count)
    ]
    return lax.ppermute(value, ("gx", "gy"), pairs)


def exact_log2(value):
    assert value & (value - 1) == 0
    return value.bit_length() - 1


def look_up(table, index):
    packed = sum(value << (3 * place) for place, value in enumerate(table))
    return lax.shift_right_logical(jnp.full(index.shape, packed, jnp.int32), 3 * index) & 7


def build_lists(links, work, tiles_dev, blocks, gy_count):
    own_x, own_y = lax.axis_index("gx"), lax.axis_index("gy")
    count = links.shape[0] * links.shape[2]
    tile_bits, gy_bits = exact_log2(tiles_dev), exact_log2(gy_count)
    link = jnp.concatenate([links[block] for block in range(blocks)], axis=1)
    order = lax.broadcasted_iota(jnp.int32, link.shape, 1)
    tile = order & (tiles_dev - 1)
    place = tile * blocks + lax.shift_right_logical(order, tile_bits)
    owner = lax.shift_right_logical(link, tile_bits)
    owner_x, owner_y = lax.shift_right_logical(owner, gy_bits), owner & (gy_count - 1)
    across = jnp.where(owner_x == own_x, 0, jnp.where(owner_x == (own_x ^ 1), 1, 2))
    own_row, beside = owner_y == own_y, owner_y == (own_y ^ 1)
    kind = across + jnp.where(own_row, 0, jnp.where(beside, 3, 6))
    part, slot = look_up(PART_OF, kind), look_up(SLOT_OF, kind)
    half = lax.shift_right_logical(tile, tile_bits - 1)
    code = (place - half * (count // HALVES)) * 512 + slot * tiles_dev + (link & (tiles_dev - 1)) + 1

    def ones_where(hit):
        return jnp.where(hit, 1.0, 0.0).astype(jnp.bfloat16)

    def iota(shape, dim):
        return lax.broadcasted_iota(jnp.int32, shape, dim)

    def dot(left, right):
        return jnp.dot(left, right, preferred_element_type=jnp.float32)

    def row_dot(left, right):
        return lax.dot_general(left, right, ROW_BY_ROW, preferred_element_type=jnp.float32)

    def to_even(length):
        return ((length.astype(jnp.int32) + 1) & -2).astype(jnp.float32).astype(jnp.bfloat16)

    groups, lines = PARTS * tiles_dev, LINES
    group = part * tiles_dev + tile
    in_group = iota((groups, count), 0) == group
    members = ones_where(in_group)
    before = dot(members, ones_where(iota((count, count), 0) < iota((count, count), 1)))
    lengths = dot(members, jnp.ones((count, 128), jnp.bfloat16))
    first, second = iota((groups, groups), 0), iota((groups, groups), 1)
    half_bits = tile_bits - 1
    same_list = lax.shift_right_logical(first, half_bits) == lax.shift_right_logical(second, half_bits)
    starts = dot(ones_where(same_list & (second < first)), to_even(lengths))
    rank = jnp.sum(jnp.where(in_group, before + starts[:, :1], 0.0), axis=0, keepdims=True).astype(jnp.int32)
    row = (part * HALVES + half) * LIST_ROWS + lax.shift_right_logical(rank, 7)
    column_hits = ones_where(iota((128, count), 0) == (rank & 127))
    row_hits = iota((lines, count), 0) == row
    listed = jnp.zeros((lines, 128), jnp.float32)
    for shift in (16, 8, 0):
        digit = (lax.shift_right_logical(code, shift) & 255).astype(jnp.float32)
        listed = listed * 256.0 + row_dot(jnp.where(row_hits, digit, 0.0).astype(jnp.bfloat16), column_hits)
    by_group = to_even(row_dot(jnp.ones((lines, count), jnp.bfloat16), members))
    of_list = iota((128, groups), 0) == lax.shift_right_logical(iota((128, groups), 1), half_bits)
    totals = row_dot(by_group, ones_where(of_list))
    work[...] = jnp.where(iota((lines, 128), 0) == lines - 1, totals, listed).astype(jnp.int32)


def lay_out(sources, rows, tiles_dev):
    width = rows.shape[-1]
    rows[0] = jnp.zeros(rows.shape[1:], rows.dtype)
    for slot, source in enumerate(sources):
        for tile in range(tiles_dev):
            rows[1 + slot * tiles_dev + tile] = source[:, tile * width:(tile + 1) * width]


def batches(part, half, work):
    return lax.div(work[LINES - 1, part * HALVES + half] + (UNROLL - 1), UNROLL)


def products_of(part, half, work, index, near, acc, rows):
    tiles_half = acc.shape[0] // HALVES
    blocks = near.shape[0] // tiles_half
    groups = 128 // UNROLL
    line = (part * HALVES + half) * LIST_ROWS + lax.div(index, groups)
    begin = lax.rem(index, groups) * UNROLL
    products = []
    for lane in range(0, UNROLL, 2):
        codes = [work[line, begin + lane + i] for i in range(2)]
        entries = [lax.shift_right_logical(code, 9) for code in codes]
        left = jnp.concatenate([near[entry] for entry in entries], axis=1)
        right = jnp.concatenate([rows[code & 511] for code in codes], axis=1)
        product = lax.dot_general(left, right, ROW_BY_ROW, preferred_element_type=jnp.float32)
        products.append((lax.div(entries[0], blocks) + half * tiles_half, product))
    return products


def add_all(products, acc):
    for target, product in products:
        acc[target] += product


def add_both(part, work, nears, acc, rows):
    def step(index, carry):
        products = []
        for half, near in enumerate(nears):
            products += products_of(part, half, work, index, near, acc, rows)
        add_all(products, acc)
        return carry

    longest = jnp.maximum(*(batches(part, half, work) for half in range(HALVES)))
    lax.fori_loop(0, longest, step, 0)


def loads_of(half, near_hbm, near, sems):
    length = near.shape[0] // CHUNKS
    return [
        pltpu.make_async_copy(
            near_hbm.at[pl.ds(half * near.shape[0] + chunk * length, length)],
            near.at[pl.ds(chunk * length, length)],
            sems.at[chunk],
        )
        for chunk in range(CHUNKS)
    ]


def load_kernel(tiles_dev, gy_count, links, near_hbm, near_0, near_1, work, sems):
    loads = loads_of(0, near_hbm, near_0, sems.at[0]) + loads_of(1, near_hbm, near_1, sems.at[1])[:AHEAD]
    for load in loads:
        load.start()
    build_lists(links, work, tiles_dev, near_hbm.shape[0] // tiles_dev, gy_count)
    for load in loads:
        load.wait()


def early_kernel(work_in, near_hbm, near_0, near_in, *refs):
    near_1, acc, rows, work, sem, sems = refs[-6:]
    loads = loads_of(1, near_hbm, near_1, sems)
    for load in loads[AHEAD:]:
        load.start()
    copy = pltpu.make_async_copy(work_in, work, sem)
    copy.start()
    lay_out(refs[:-6], rows, acc.shape[0])
    acc[...] = jnp.zeros(acc.shape, acc.dtype)
    copy.wait()
    length = near_1.shape[0] // CHUNKS
    count = batches(0, 1, work)

    def wait(chunk, carry):
        held = near_1.at[pl.ds(chunk * length, length)]
        pltpu.make_async_copy(near_hbm.at[pl.ds(chunk * length, length)], held, sems.at[chunk]).wait()
        return carry

    def step(pair, there):
        groups = 128 // UNROLL
        index = 2 * pair + 1
        last = work[LIST_ROWS + lax.div(index, groups), lax.rem(index, groups) * UNROLL + UNROLL - 2]
        needed = jnp.where(index >= count - 1, CHUNKS, lax.div(lax.shift_right_logical(last, 9), length) + 1)
        lax.fori_loop(there, needed, wait, 0)
        products = []
        for place in (index - 1, index):
            for half, near in enumerate((near_0, near_1)):
                products += products_of(0, half, work, place, near, acc, rows)
        add_all(products, acc)
        return jnp.maximum(there, needed)

    pairs = lax.div(jnp.maximum(batches(0, 0, work), count) + 1, 2)
    there = lax.fori_loop(0, pairs, step, jnp.int32(AHEAD))
    lax.fori_loop(there, CHUNKS, wait, 0)


def next_kernel(work_in, near_0, near_1, *refs):
    acc, rows, work, sem = refs[-4:]
    copy = pltpu.make_async_copy(work_in, work, sem)
    copy.start()
    lay_out(refs[:-5], rows, acc.shape[0])
    copy.wait()
    add_both(1, work, (near_0, near_1), acc, rows)


def last_kernel(work_in, near_0, near_1, outer, core, acc_in, split, gram, acc, rows, work, sem):
    tiles_dev, width, columns = acc.shape
    copy = pltpu.make_async_copy(work_in, work, sem)
    copy.start()
    lay_out((outer, core), rows, tiles_dev)
    copy.wait()
    add_both(2, work, (near_0, near_1), acc, rows)
    for tile in range(tiles_dev):
        image = acc[tile].T
        high = image.astype(jnp.bfloat16)
        low = (image - high.astype(jnp.float32)).astype(jnp.bfloat16)
        split[:, tile * width:(tile + 1) * width] = jnp.concatenate([high, low], axis=0)
    both = split[...]
    full = lax.dot_general(both, both, ROW_BY_ROW, preferred_element_type=jnp.float32)
    top = full[:columns, :columns] + full[columns:, columns:]
    side = full[:columns, columns:] + full[columns:, :columns]
    total = top + side
    gram[...] = jnp.concatenate([total[:columns // 2], total[columns // 2:]], axis=1)


def finish_kernel(scale, gram, split, basis, factor):
    columns = 2 * gram.shape[0]
    shape = (8, 2 * columns)
    row = lax.broadcasted_iota(jnp.int32, shape, 0)
    lane = lax.broadcasted_iota(jnp.int32, shape, 1)
    groups = columns // 8
    live = []
    for g in range(groups):
        unit = jnp.where(lane == row + (columns + 8 * g), 1.0, 0.0)
        begin, side = 8 * g % (columns // 2), 8 * g // (columns // 2) * columns
        live.append(jnp.concatenate([gram[begin:begin + 8, side:side + columns], unit[:, columns:]], axis=1))
    done = []
    for g in range(groups):
        cols = [[jnp.broadcast_to(part[:, 8 * g + j:8 * g + j + 1], shape) for part in live] for j in range(8)]
        pivots = jnp.ones(shape, jnp.float32)
        for j in range(8):
            pivot = jnp.broadcast_to(cols[j][0][j:j+1], shape)
            pivots = jnp.where(row == j, pivot, pivots)
            inverse = 1.0 / pivot
            ratios = [part * inverse for part in cols[j]]
            ratios[0] = jnp.where(row > j, ratios[0], 0.0)
            for i in range(j + 1, 8):
                pick = jnp.broadcast_to(cols[i][0][j:j+1], shape)
                cols[i] = [part - ratio * pick for part, ratio in zip(cols[i], ratios)]
            pick = jnp.broadcast_to(live[0][j:j+1], shape)
            live = [part - ratio * pick for part, ratio in zip(live, ratios)]
        done.append(live[0] * lax.rsqrt(pivots))
        live = live[1:]
    whole = jnp.concatenate(done, axis=0)
    left, right = whole[:, :columns], whole[:, columns:]
    on_or_above = lax.broadcasted_iota(jnp.int32, left.shape, 0) <= lax.broadcasted_iota(jnp.int32, left.shape, 1)
    factor[...] = jnp.where(on_or_above, left, 0.0) * (1.0 / scale)
    weight = right * scale
    high = weight.astype(jnp.bfloat16)
    low = (weight - high.astype(jnp.float32)).astype(jnp.bfloat16)
    stacked = jnp.concatenate([high, high, low], axis=1)
    values = jnp.concatenate([split[...], split[:columns]], axis=0)
    basis[...] = jnp.dot(stacked, values, preferred_element_type=jnp.float32)


def in_vmem():
    return pl.BlockSpec(memory_space=pltpu.VMEM)


def sum_over_all(value):
    gx_count, gy_count = lax.axis_size("gx"), lax.axis_size("gy")
    total = gx_count * gy_count
    bits = [gy_count * 2**i for i in range(1, gx_count.bit_length() - 1)]
    along = [2**i for i in range(gy_count.bit_length() - 1)]
    bits = bits[:1] + along[1:2] + along[:1] + along[2:] + bits[1:]

    def from_other(mask):
        return lax.ppermute(value, ("gx", "gy"), [(i, i ^ mask) for i in range(total)])

    value = value + from_other(gy_count)
    while bits:
        taken, bits = bits[:2], bits[2:]
        near = value + from_other(taken[0])
        if len(taken) == 2:
            near = near + (from_other(taken[1]) + from_other(taken[0] ^ taken[1]))
        value = near
    return value


def shards(near_tiles, block, adjacency):
    tiles_dev, blocks = adjacency.shape[2:]
    width = near_tiles.shape[4]
    rows, columns = block.shape[2:]
    gx_count, gy_count = lax.axis_size("gx"), lax.axis_size("gy")
    scale = float(rows * gx_count * gy_count) ** 0.5

    beside = pair_swap(block, "gy")
    two_off = to_mate_of_outside(block)
    outer = between_pairs(block, "gx")
    core = pair_swap(block, "gx")

    count = tiles_dev * blocks
    links = adjacency[0, 0].T.reshape(blocks, 1, tiles_dev)
    near = near_tiles.reshape(count, width, width)
    acc_shape = jax.ShapeDtypeStruct((tiles_dev, width, columns), jnp.float32)
    flat = lambda value: value[0, 0].T

    def tile_rows(sources):
        return pltpu.VMEM((sources * tiles_dev + 1, columns, width), jnp.bfloat16)

    def params(limit=VMEM_LIMIT):
        return dict(
            compiler_params=pltpu.CompilerParams(vmem_limit_bytes=limit),
        )

    work_scratch = [pltpu.SMEM((LINES, 128), jnp.int32), pltpu.SemaphoreType.DMA]
    near_half = pltpu.VMEM((count // HALVES, width, width), near.dtype)
    near_0, near_1, work = pl.pallas_call(
        functools.partial(load_kernel, tiles_dev, gy_count),
        out_shape=(near_half, near_half, jax.ShapeDtypeStruct((LINES, 128), jnp.int32)),
        in_specs=[in_vmem(), pl.BlockSpec(memory_space=pltpu.HBM)], out_specs=(in_vmem(),) * 3,
        scratch_shapes=[pltpu.SemaphoreType.DMA((HALVES, CHUNKS))], name="load", **params(24 * 2**20),
    )(links, near)

    beside, two_off, work = lax.optimization_barrier((beside, two_off, work))
    beyond = pass_on(beside, "gy")
    beside_outer = swap_of_outer(outer)
    beyond_outer = from_mate_across(two_off)
    beside_core = pair_swap(beside, "gx")
    sources = (block, core, outer, beside, beside_core)
    near_1, acc = pl.pallas_call(
        early_kernel, out_shape=(near_half, acc_shape),
        in_specs=[in_vmem(), pl.BlockSpec(memory_space=pltpu.HBM)] + [in_vmem()] * 7, out_specs=(in_vmem(),) * 2,
        scratch_shapes=[tile_rows(5)] + work_scratch + [pltpu.SemaphoreType.DMA((CHUNKS,))],
        name="early_rows", input_output_aliases={3: 0}, **params(24 * 2**20),
    )(work, near, near_0, near_1, *(flat(source) for source in sources))

    beyond, beyond_outer, acc = lax.optimization_barrier((beyond, beyond_outer, acc))
    beyond_core = pair_swap(beyond, "gx")
    acc = pl.pallas_call(
        next_kernel, out_shape=acc_shape, in_specs=[in_vmem()] * 6, out_specs=in_vmem(),
        scratch_shapes=[tile_rows(2)] + work_scratch, name="next_rows", input_output_aliases={5: 0}, **params(),
    )(work, near_0, near_1, flat(beyond), flat(beyond_outer), acc)

    beside_outer, beyond_core, acc = lax.optimization_barrier((beside_outer, beyond_core, acc))
    split, gram, _ = pl.pallas_call(
        last_kernel,
        out_shape=(
            jax.ShapeDtypeStruct((2 * columns, rows), jnp.bfloat16),
            jax.ShapeDtypeStruct((columns // 2, 2 * columns), jnp.float32),
            acc_shape,
        ),
        in_specs=[in_vmem()] * 6, out_specs=(in_vmem(),) * 3,
        scratch_shapes=[tile_rows(2)] + work_scratch, name="last_rows_and_gram", input_output_aliases={5: 2}, **params(),
    )(work, near_0, near_1, flat(beside_outer), flat(beyond_core), acc)

    gram = sum_over_all(gram)
    basis, factor = pl.pallas_call(
        functools.partial(finish_kernel, scale),
        out_shape=(
            jax.ShapeDtypeStruct((columns, rows), jnp.float32),
            jax.ShapeDtypeStruct((columns, columns), jnp.float32),
        ),
        in_specs=[in_vmem()] * 2, out_specs=(in_vmem(), in_vmem()), name="orthonormalize", **params(),
    )(gram, split)
    return basis.T.reshape(1, 1, rows, columns), factor


def solution(mesh):
    in_specs = (
        P("gx", "gy", None, None, None, None),
        P("gx", "gy", None, None),
        P("gx", "gy", None, None),
    )
    out_specs = (P("gx", "gy", None, None), P())
    return jax.shard_map(shards, mesh=mesh, in_specs=in_specs, out_specs=out_specs, check_vma=False)
```

```python
import functools

import jax
import jax.numpy as jnp
from jax import lax
from jax.experimental import pallas as pl
from jax.experimental.pallas import tpu as pltpu
from jax.sharding import PartitionSpec as P

UNROLL = 32
PARTS = 3
HALVES = 2
CHUNKS = 4
AHEAD = 1
LIST_ROWS = 3
LINES = PARTS * HALVES * LIST_ROWS + 6
PART_OF = (0, 0, 0, 0, 0, 2, 1, 2, 1)
SLOT_OF = (0, 1, 2, 3, 4, 0, 0, 1, 1)
ROW_BY_ROW = (((1,), (1,)), ((), ()))
VMEM_LIMIT = 8 * 2**20


def pair_swap(value, axis):
    size = lax.axis_size(axis)
    return lax.ppermute(value, axis, [(i, i ^ 1) for i in range(size)])


def between_pairs(value, axis):
    return lax.ppermute(value, axis, outside(lax.axis_size(axis)))


def outside(size):
    return [(i, i + 1) for i in range(1, size - 1, 2)] + [(i + 1, i) for i in range(1, size - 1, 2)]


def pass_on(value, axis):
    pairs = [(sender ^ 1, receiver) for sender, receiver in outside(lax.axis_size(axis))]
    return lax.ppermute(value, axis, pairs)


def swap_of_outer(value):
    gx_count, gy_count = lax.axis_size("gx"), lax.axis_size("gy")
    pairs = [(x * gy_count + y, x * gy_count + (y ^ 1)) for x, _ in outside(gx_count) for y in range(gy_count)]
    return lax.ppermute(value, ("gx", "gy"), pairs)


def to_mate_of_outside(value):
    gx_count, gy_count = lax.axis_size("gx"), lax.axis_size("gy")
    pairs = [
        (x * gy_count + sender, x * gy_count + (receiver ^ 1))
        for x, _ in outside(gx_count)
        for sender, receiver in outside(gy_count)
    ]
    return lax.ppermute(value, ("gx", "gy"), pairs)


def from_mate_across(value):
    gx_count, gy_count = lax.axis_size("gx"), lax.axis_size("gy")
    pairs = [
        (from_x * gy_count + (receiver ^ 1), to_x * gy_count + receiver)
        for from_x, to_x in outside(gx_count)
        for _, receiver in outside(gy_count)
    ]
    return lax.ppermute(value, ("gx", "gy"), pairs)


def exact_log2(value):
    assert value & (value - 1) == 0
    return value.bit_length() - 1


def look_up(table, index):
    packed = sum(value << (3 * place) for place, value in enumerate(table))
    return lax.shift_right_logical(jnp.full(index.shape, packed, jnp.int32), 3 * index) & 7


def build_lists(links, work, tiles_dev, blocks, gy_count):
    own_x, own_y = lax.axis_index("gx"), lax.axis_index("gy")
    count = links.shape[0] * links.shape[2]
    tile_bits, gy_bits = exact_log2(tiles_dev), exact_log2(gy_count)
    link = jnp.concatenate([links[block] for block in range(blocks)], axis=1)
    order = lax.broadcasted_iota(jnp.int32, link.shape, 1)
    tile = order & (tiles_dev - 1)
    place = tile * blocks + lax.shift_right_logical(order, tile_bits)
    owner = lax.shift_right_logical(link, tile_bits)
    owner_x, owner_y = lax.shift_right_logical(owner, gy_bits), owner & (gy_count - 1)
    across = jnp.where(owner_x == own_x, 0, jnp.where(owner_x == (own_x ^ 1), 1, 2))
    own_row, beside = owner_y == own_y, owner_y == (own_y ^ 1)
    kind = across + jnp.where(own_row, 0, jnp.where(beside, 3, 6))
    part, slot = look_up(PART_OF, kind), look_up(SLOT_OF, kind)
    half = lax.shift_right_logical(tile, tile_bits - 1)
    code = (place - half * (count // HALVES)) * 512 + slot * tiles_dev + (link & (tiles_dev - 1)) + 1

    def ones_where(hit):
        return jnp.where(hit, 1.0, 0.0).astype(jnp.bfloat16)

    def iota(shape, dim):
        return lax.broadcasted_iota(jnp.int32, shape, dim)

    def dot(left, right):
        return jnp.dot(left, right, preferred_element_type=jnp.float32)

    def row_dot(left, right):
        return lax.dot_general(left, right, ROW_BY_ROW, preferred_element_type=jnp.float32)

    def to_even(length):
        return ((length.astype(jnp.int32) + 1) & -2).astype(jnp.float32).astype(jnp.bfloat16)

    groups, lines = PARTS * tiles_dev, LINES
    group = part * tiles_dev + tile
    in_group = iota((groups, count), 0) == group
    members = ones_where(in_group)
    before = dot(members, ones_where(iota((count, count), 0) < iota((count, count), 1)))
    lengths = dot(members, jnp.ones((count, 128), jnp.bfloat16))
    first, second = iota((groups, groups), 0), iota((groups, groups), 1)
    half_bits = tile_bits - 1
    same_list = lax.shift_right_logical(first, half_bits) == lax.shift_right_logical(second, half_bits)
    starts = dot(ones_where(same_list & (second < first)), to_even(lengths))
    rank = jnp.sum(jnp.where(in_group, before + starts[:, :1], 0.0), axis=0, keepdims=True).astype(jnp.int32)
    row = (part * HALVES + half) * LIST_ROWS + lax.shift_right_logical(rank, 7)
    column_hits = ones_where(iota((128, count), 0) == (rank & 127))
    row_hits = iota((lines, count), 0) == row
    listed = jnp.zeros((lines, 128), jnp.float32)
    for shift in (16, 8, 0):
        digit = (lax.shift_right_logical(code, shift) & 255).astype(jnp.float32)
        listed = listed * 256.0 + row_dot(jnp.where(row_hits, digit, 0.0).astype(jnp.bfloat16), column_hits)
    by_group = to_even(row_dot(jnp.ones((lines, count), jnp.bfloat16), members))
    of_list = iota((128, groups), 0) == lax.shift_right_logical(iota((128, groups), 1), half_bits)
    totals = row_dot(by_group, ones_where(of_list))
    work[...] = jnp.where(iota((lines, 128), 0) == lines - 1, totals, listed).astype(jnp.int32)


def lay_out(sources, rows, tiles_dev):
    width = rows.shape[-1]
    rows[0] = jnp.zeros(rows.shape[1:], rows.dtype)
    for slot, source in enumerate(sources):
        for tile in range(tiles_dev):
            rows[1 + slot * tiles_dev + tile] = source[:, tile * width:(tile + 1) * width]


def batches(part, half, work):
    return lax.div(work[LINES - 1, part * HALVES + half] + (UNROLL - 1), UNROLL)


def products_of(part, half, work, index, near, acc, rows):
    tiles_half = acc.shape[0] // HALVES
    blocks = near.shape[0] // tiles_half
    groups = 128 // UNROLL
    line = (part * HALVES + half) * LIST_ROWS + lax.div(index, groups)
    begin = lax.rem(index, groups) * UNROLL
    products = []
    for lane in range(0, UNROLL, 2):
        codes = [work[line, begin + lane + i] for i in range(2)]
        entries = [lax.shift_right_logical(code, 9) for code in codes]
        left = jnp.concatenate([near[entry] for entry in entries], axis=1)
        right = jnp.concatenate([rows[code & 511] for code in codes], axis=1)
        product = lax.dot_general(left, right, ROW_BY_ROW, preferred_element_type=jnp.float32)
        products.append((lax.div(entries[0], blocks) + half * tiles_half, product))
    return products


def add_all(products, acc):
    for target, product in products:
        acc[target] += product


def add_both(part, work, nears, acc, rows):
    def step(index, carry):
        products = []
        for half, near in enumerate(nears):
            products += products_of(part, half, work, index, near, acc, rows)
        add_all(products, acc)
        return carry

    longest = jnp.maximum(*(batches(part, half, work) for half in range(HALVES)))
    lax.fori_loop(0, longest, step, 0)


def loads_of(half, near_hbm, near, sems):
    length = near.shape[0] // CHUNKS
    return [
        pltpu.make_async_copy(
            near_hbm.at[pl.ds(half * near.shape[0] + chunk * length, length)],
            near.at[pl.ds(chunk * length, length)],
            sems.at[chunk],
        )
        for chunk in range(CHUNKS)
    ]


def load_kernel(tiles_dev, gy_count, links, near_hbm, near_0, near_1, work, sems):
    loads = loads_of(0, near_hbm, near_0, sems.at[0]) + loads_of(1, near_hbm, near_1, sems.at[1])[:AHEAD]
    for load in loads:
        load.start()
    build_lists(links, work, tiles_dev, near_hbm.shape[0] // tiles_dev, gy_count)
    for load in loads:
        load.wait()


def early_kernel(work_in, near_hbm, near_0, near_in, *refs):
    near_1, acc, rows, work, sem, sems = refs[-6:]
    loads = loads_of(1, near_hbm, near_1, sems)
    for load in loads[AHEAD:]:
        load.start()
    copy = pltpu.make_async_copy(work_in, work, sem)
    copy.start()
    lay_out(refs[:-6], rows, acc.shape[0])
    acc[...] = jnp.zeros(acc.shape, acc.dtype)
    copy.wait()
    length = near_1.shape[0] // CHUNKS
    count = batches(0, 1, work)

    def wait(chunk, carry):
        held = near_1.at[pl.ds(chunk * length, length)]
        pltpu.make_async_copy(near_hbm.at[pl.ds(chunk * length, length)], held, sems.at[chunk]).wait()
        return carry

    def step(index, there):
        groups = 128 // UNROLL
        last = work[LIST_ROWS + lax.div(index, groups), lax.rem(index, groups) * UNROLL + UNROLL - 2]
        needed = jnp.where(index >= count - 1, CHUNKS, lax.div(lax.shift_right_logical(last, 9), length) + 1)
        lax.fori_loop(there, needed, wait, 0)
        products = []
        for half, near in enumerate((near_0, near_1)):
            products += products_of(0, half, work, index, near, acc, rows)
        add_all(products, acc)
        return jnp.maximum(there, needed)

    there = lax.fori_loop(0, jnp.maximum(batches(0, 0, work), count), step, jnp.int32(AHEAD))
    lax.fori_loop(there, CHUNKS, wait, 0)


def next_kernel(work_in, near_0, near_1, *refs):
    acc, rows, work, sem = refs[-4:]
    copy = pltpu.make_async_copy(work_in, work, sem)
    copy.start()
    lay_out(refs[:-5], rows, acc.shape[0])
    copy.wait()
    add_both(1, work, (near_0, near_1), acc, rows)


def last_kernel(work_in, near_0, near_1, outer, core, acc_in, split, gram, acc, rows, work, sem):
    tiles_dev, width, columns = acc.shape
    copy = pltpu.make_async_copy(work_in, work, sem)
    copy.start()
    lay_out((outer, core), rows, tiles_dev)
    copy.wait()
    add_both(2, work, (near_0, near_1), acc, rows)
    for tile in range(tiles_dev):
        image = acc[tile].T
        high = image.astype(jnp.bfloat16)
        low = (image - high.astype(jnp.float32)).astype(jnp.bfloat16)
        split[:, tile * width:(tile + 1) * width] = jnp.concatenate([high, low], axis=0)
    both = split[...]
    full = lax.dot_general(both, both, ROW_BY_ROW, preferred_element_type=jnp.float32)
    top = full[:columns, :columns] + full[columns:, columns:]
    side = full[:columns, columns:] + full[columns:, :columns]
    total = top + side
    gram[...] = jnp.concatenate([total[:columns // 2], total[columns // 2:]], axis=1)


def finish_kernel(scale, gram, split, basis, factor):
    columns = 2 * gram.shape[0]
    shape = (8, 2 * columns)
    row = lax.broadcasted_iota(jnp.int32, shape, 0)
    lane = lax.broadcasted_iota(jnp.int32, shape, 1)
    groups = columns // 8
    live = []
    for g in range(groups):
        unit = jnp.where(lane == row + (columns + 8 * g), 1.0, 0.0)
        begin, side = 8 * g % (columns // 2), 8 * g // (columns // 2) * columns
        live.append(jnp.concatenate([gram[begin:begin + 8, side:side + columns], unit[:, columns:]], axis=1))
    done = []
    for g in range(groups):
        cols = [[jnp.broadcast_to(part[:, 8 * g + j:8 * g + j + 1], shape) for part in live] for j in range(8)]
        pivots = jnp.ones(shape, jnp.float32)
        for j in range(8):
            pivot = jnp.broadcast_to(cols[j][0][j:j+1], shape)
            pivots = jnp.where(row == j, pivot, pivots)
            inverse = 1.0 / pivot
            ratios = [part * inverse for part in cols[j]]
            ratios[0] = jnp.where(row > j, ratios[0], 0.0)
            for i in range(j + 1, 8):
                pick = jnp.broadcast_to(cols[i][0][j:j+1], shape)
                cols[i] = [part - ratio * pick for part, ratio in zip(cols[i], ratios)]
            pick = jnp.broadcast_to(live[0][j:j+1], shape)
            live = [part - ratio * pick for part, ratio in zip(live, ratios)]
        done.append(live[0] * lax.rsqrt(pivots))
        live = live[1:]
    whole = jnp.concatenate(done, axis=0)
    left, right = whole[:, :columns], whole[:, columns:]
    on_or_above = lax.broadcasted_iota(jnp.int32, left.shape, 0) <= lax.broadcasted_iota(jnp.int32, left.shape, 1)
    factor[...] = jnp.where(on_or_above, left, 0.0) * (1.0 / scale)
    weight = right * scale
    high = weight.astype(jnp.bfloat16)
    low = (weight - high.astype(jnp.float32)).astype(jnp.bfloat16)
    stacked = jnp.concatenate([high, high, low], axis=1)
    values = jnp.concatenate([split[...], split[:columns]], axis=0)
    basis[...] = jnp.dot(stacked, values, preferred_element_type=jnp.float32)


def in_vmem():
    return pl.BlockSpec(memory_space=pltpu.VMEM)


def sum_over_all(value):
    gx_count, gy_count = lax.axis_size("gx"), lax.axis_size("gy")
    total = gx_count * gy_count
    bits = [gy_count * 2**i for i in range(1, gx_count.bit_length() - 1)]
    bits = bits[:1] + [2**i for i in range(gy_count.bit_length() - 1)] + bits[1:]

    def from_other(mask):
        return lax.ppermute(value, ("gx", "gy"), [(i, i ^ mask) for i in range(total)])

    value = value + from_other(gy_count)
    while bits:
        taken, bits = bits[:2], bits[2:]
        near = value + from_other(taken[0])
        if len(taken) == 2:
            near = near + (from_other(taken[1]) + from_other(taken[0] ^ taken[1]))
        value = near
    return value


def shards(near_tiles, block, adjacency):
    tiles_dev, blocks = adjacency.shape[2:]
    width = near_tiles.shape[4]
    rows, columns = block.shape[2:]
    gx_count, gy_count = lax.axis_size("gx"), lax.axis_size("gy")
    scale = float(rows * gx_count * gy_count) ** 0.5

    beside = pair_swap(block, "gy")
    two_off = to_mate_of_outside(block)
    outer = between_pairs(block, "gx")
    core = pair_swap(block, "gx")

    count = tiles_dev * blocks
    links = adjacency[0, 0].T.reshape(blocks, 1, tiles_dev)
    near = near_tiles.reshape(count, width, width)
    acc_shape = jax.ShapeDtypeStruct((tiles_dev, width, columns), jnp.float32)
    flat = lambda value: value[0, 0].T

    def tile_rows(sources):
        return pltpu.VMEM((sources * tiles_dev + 1, columns, width), jnp.bfloat16)

    def params(limit=VMEM_LIMIT):
        return dict(
            compiler_params=pltpu.CompilerParams(vmem_limit_bytes=limit),
        )

    work_scratch = [pltpu.SMEM((LINES, 128), jnp.int32), pltpu.SemaphoreType.DMA]
    near_half = pltpu.VMEM((count // HALVES, width, width), near.dtype)
    near_0, near_1, work = pl.pallas_call(
        functools.partial(load_kernel, tiles_dev, gy_count),
        out_shape=(near_half, near_half, jax.ShapeDtypeStruct((LINES, 128), jnp.int32)),
        in_specs=[in_vmem(), pl.BlockSpec(memory_space=pltpu.HBM)], out_specs=(in_vmem(),) * 3,
        scratch_shapes=[pltpu.SemaphoreType.DMA((HALVES, CHUNKS))], name="load", **params(24 * 2**20),
    )(links, near)

    beside, two_off, work = lax.optimization_barrier((beside, two_off, work))
    beyond = pass_on(beside, "gy")
    beside_outer = swap_of_outer(outer)
    beyond_outer = from_mate_across(two_off)
    beside_core = pair_swap(beside, "gx")
    sources = (block, core, outer, beside, beside_core)
    near_1, acc = pl.pallas_call(
        early_kernel, out_shape=(near_half, acc_shape),
        in_specs=[in_vmem(), pl.BlockSpec(memory_space=pltpu.HBM)] + [in_vmem()] * 7, out_specs=(in_vmem(),) * 2,
        scratch_shapes=[tile_rows(5)] + work_scratch + [pltpu.SemaphoreType.DMA((CHUNKS,))],
        name="early_rows", input_output_aliases={3: 0}, **params(24 * 2**20),
    )(work, near, near_0, near_1, *(flat(source) for source in sources))

    beyond, beyond_outer, acc = lax.optimization_barrier((beyond, beyond_outer, acc))
    beyond_core = pair_swap(beyond, "gx")
    acc = pl.pallas_call(
        next_kernel, out_shape=acc_shape, in_specs=[in_vmem()] * 6, out_specs=in_vmem(),
        scratch_shapes=[tile_rows(2)] + work_scratch, name="next_rows", input_output_aliases={5: 0}, **params(),
    )(work, near_0, near_1, flat(beyond), flat(beyond_outer), acc)

    beside_outer, beyond_core, acc = lax.optimization_barrier((beside_outer, beyond_core, acc))
    split, gram, _ = pl.pallas_call(
        last_kernel,
        out_shape=(
            jax.ShapeDtypeStruct((2 * columns, rows), jnp.bfloat16),
            jax.ShapeDtypeStruct((columns // 2, 2 * columns), jnp.float32),
            acc_shape,
        ),
        in_specs=[in_vmem()] * 6, out_specs=(in_vmem(),) * 3,
        scratch_shapes=[tile_rows(2)] + work_scratch, name="last_rows_and_gram", input_output_aliases={5: 2}, **params(),
    )(work, near_0, near_1, flat(beside_outer), flat(beyond_core), acc)

    gram = sum_over_all(gram)
    basis, factor = pl.pallas_call(
        functools.partial(finish_kernel, scale),
        out_shape=(
            jax.ShapeDtypeStruct((columns, rows), jnp.float32),
            jax.ShapeDtypeStruct((columns, columns), jnp.float32),
        ),
        in_specs=[in_vmem()] * 2, out_specs=(in_vmem(), in_vmem()), name="orthonormalize", **params(),
    )(gram, split)
    return basis.T.reshape(1, 1, rows, columns), factor


def solution(mesh):
    in_specs = (
        P("gx", "gy", None, None, None, None),
        P("gx", "gy", None, None),
        P("gx", "gy", None, None),
    )
    out_specs = (P("gx", "gy", None, None), P())
    return jax.shard_map(shards, mesh=mesh, in_specs=in_specs, out_specs=out_specs, check_vma=False)
```
